32 devices in a mesh: ctx: 8 (over y, x, core), dp: 4 (over z).
Axes of the slice: x: 2, y: 2, z: 4, core: 2. Of those that a mesh axis runs over, the one named last changes fastest.
Arguments:
- queries: bfloat16 [4, 1024, 1536], P('dp', 'ctx'), as said below
- keys: bfloat16 [4, 1024, 1536], P('dp', 'ctx'), as said below
- values: bfloat16 [4, 1024, 1536], P('dp', 'ctx'), may hold values from -6 to 6
- tangent_queries: bfloat16 [4, 1024, 1536], P('dp', 'ctx'), may hold values from -6 to 6
- tangent_keys: bfloat16 [4, 1024, 1536], P('dp', 'ctx'), may hold values from -6 to 6
- tangent_values: bfloat16 [4, 1024, 1536], P('dp', 'ctx'), may hold values from -6 to 6
- clip_ids: int32 [4, 1024], P('dp', 'ctx'), may hold values from 0 to 3, never falling along the last dimension, each value on 1 to 512 neighbouring positions
- block_order: int32 [8], replicated, may hold values from 0 to 7, each once
- out_weight: bfloat16 [1536, 3072], replicated, may hold values from -0.15625 to 0.15625
- layer_scale: float32 [3072], replicated, may hold values from 0.1 to 1.9
- cotangent: bfloat16 [4, 1024, 3072], P('dp', 'ctx'), as said below
Outputs:
- tangent_branch: bfloat16 [4, 1024, 3072], P('dp', 'ctx')
- scale_grad: float32 [3072], replicated
The draws below stay inside these ranges and needn't reach their ends.
Inputs may be any that keep to these rules, and one draw needn't show every extreme that they name: `clip_ids`: ids never fall along a sample's rows; each of the 4 clips is a run of consecutive rows. `block_order`: each block number appears once. `queries`: real-valued. `keys`: real-valued. `cotangent`: real-valued.
All inputs are finite; a program needn't handle non-finite values.
Results may differ from the reference program's by a relative error of at most 0.02.
The reference program's roundings to bfloat16 on the way count: a program that leaves them out, or rounds other values in their place, can miss the bound.
Values may be sent and summed in bfloat16 or wider, within the bound.
No kernel may reach another device: no remote copies, remote signals or barrier semaphores. Data moves between devices by JAX's collectives and lax.ppermute only.
A program may use at most 192 MiB of HBM per device.

```python
import math
import jax
import jax.numpy as jnp
import numpy as np
from jax import lax

D = 3072
HEADS = 12
HD = 128
TOK_DEV = 128
CLIPS = 4
HW = 1536
SEQ = 1024
SAMPLES = 4
N_CTX = 8


def qk_draw(key, which):
    noise = jax.random.normal(jax.random.fold_in(key, 101 + which), (SAMPLES, SEQ, HEADS * HD), jnp.float32)
    return noise.astype(jnp.bfloat16)


def draw_queries(key, part):
    return qk_draw(key, 0)


def draw_keys(key, part):
    return qk_draw(key, 1)


def draw_cotangent(key, part):
    noise = jax.random.normal(jax.random.fold_in(key, 301), (SAMPLES, SEQ, D), jnp.float32)
    row_scale = jnp.exp(jax.random.uniform(jax.random.fold_in(key, 302), (SAMPLES, SEQ, 1), jnp.float32, 0.0, math.log(10.0)))
    col_scale = jnp.exp(jax.random.uniform(jax.random.fold_in(key, 303), (1, 1, D), jnp.float32, 0.0, math.log(10.0)))
    along_seq = 1.0 + 2.0 * jnp.arange(SEQ, dtype=jnp.float32) / SEQ
    along_samples = 1.0 + 2.0 * jnp.arange(SAMPLES, dtype=jnp.float32) / max(SAMPLES - 1, 1)
    rising = along_samples[:, None, None] * along_seq[None, :, None]
    return (noise * row_scale * col_scale * rising / 30.0).astype(jnp.bfloat16)


def block_scale(stream_key, dims, shards, low, top_value):
    loudness, own = 1.0, jax.random.fold_in(stream_key, 6)
    for axis_at, shards_of in shards:
        draws = jnp.exp(jax.random.uniform(jax.random.fold_in(own, axis_at), (shards_of,), jnp.float32, low / len(shards), top_value / len(shards)))
        loudness = loudness * jnp.repeat(draws, dims[axis_at] // shards_of).reshape([-1 if axis == axis_at else 1 for axis in range(len(dims))])
    return loudness


def split_up(number_of, total, reach, slope):
    weights = [(1 << 20) // math.isqrt(rank ** slope) + 1 for rank in range(2, number_of + 1)]
    rest, counts = total - reach - (number_of - 1), [1] * (number_of - 1)
    while rest > 0:
        movable = [i for i in range(number_of - 1) if counts[i] < reach]
        pool, left = sum([weights[i] for i in movable]), rest
        for i in movable:
            addition = min(reach - counts[i], max(1, left * weights[i] // pool), rest)
            counts[i] = counts[i] + addition
            rest = rest - addition
    return np.array([reach] + counts)


def uneven(rng, count, total, reach, lean):
    if count == 2:
        one = jax.random.randint(rng, (), max(1, total - reach), min(reach, total - 1) + 1)
        return jnp.stack([one, total - one])
    tallies = jnp.asarray(split_up(count, total, reach, lean), jnp.int32)
    couples = (count - 1) // 2
    donor, receiver = tallies[1:1 + 2 * couples:2], tallies[2:2 + 2 * couples:2]
    slack = jnp.minimum(donor - 1, reach - receiver)
    moved = jax.random.randint(jax.random.fold_in(rng, 1), (couples,), 0, 1 << 20) % (slack + 1)
    tallies = tallies.at[1:1 + 2 * couples:2].set(donor - moved).at[2:2 + 2 * couples:2].set(receiver + moved)
    return tallies[jax.random.permutation(jax.random.fold_in(rng, 2), count)]


def bell_draw(own_key, dims, scale, bound, cuts=(), held_as=jnp.bfloat16):
    values = jax.random.normal(own_key, dims, jnp.float32) * scale
    if len(cuts) > 0:
        values = block_scale(own_key, dims, cuts, -0.22, 0.18) * values
    return jnp.clip(values, min=-bound, max=bound).astype(held_as)


def setup_inputs(seed: int = 0) -> dict:
    seeds = jax.random.split(jax.random.key(seed), 12)
    queries = draw_queries(jax.random.fold_in(seeds[11], 71), 0)
    keys = draw_keys(jax.random.fold_in(seeds[11], 71), 0)
    values = bell_draw(seeds[2], (SAMPLES, SEQ, HW), 1.0, 6.0, ((0, 4), (1, 8)))
    tangent_queries = bell_draw(seeds[3], (SAMPLES, SEQ, HW), 1.0, 6.0, ((0, 4), (1, 8)))
    tangent_keys = bell_draw(seeds[4], (SAMPLES, SEQ, HW), 1.0, 6.0, ((0, 4), (1, 8)))
    tangent_values = bell_draw(seeds[5], (SAMPLES, SEQ, HW), 1.0, 6.0, ((0, 4), (1, 8)))
    clip_ids = jax.vmap(lambda own: jnp.searchsorted(jnp.cumsum(uneven(own, CLIPS, SEQ, SEQ // 2, 2)), jnp.arange(SEQ), side="right"))(jax.random.split(seeds[6], SAMPLES)).reshape((SAMPLES, SEQ)).astype(jnp.int32)
    block_order = jax.random.permutation(seeds[7], N_CTX).astype(jnp.int32)
    out_weight = bell_draw(seeds[8], (HW, D), HW ** -0.5, 0.15625)
    layer_scale = jnp.clip(1.0 + 0.18 * jax.random.normal(seeds[9], (D,), jnp.float32), 0.1, 1.9)
    cotangent = draw_cotangent(jax.random.fold_in(seeds[11], 71), 0)
    return {"queries": queries, "keys": keys, "values": values, "tangent_queries": tangent_queries, "tangent_keys": tangent_keys, "tangent_values": tangent_values, "clip_ids": clip_ids, "block_order": block_order, "out_weight": out_weight, "layer_scale": layer_scale, "cotangent": cotangent}


def rotate(x, pos, half_dim):
    frequency = 10000.0 ** (-jnp.arange(half_dim, dtype=jnp.float32) / half_dim)
    angles = pos.astype(jnp.float32)[:, None] * frequency[None, :]
    cosine = jnp.cos(angles)[:, None, :]
    sine_part = jnp.sin(angles)[:, None, :]
    front_part = x[..., :half_dim]
    back_part = x[..., half_dim:]
    return jnp.concatenate([front_part * cosine - back_part * sine_part, back_part * cosine + front_part * sine_part], axis=-1)

def reference(queries, keys, values, tangent_queries, tangent_keys, tangent_values, clip_ids, block_order, out_weight, layer_scale, cotangent):
    seq_len = queries.shape[1]
    heads = HEADS
    head_dim = HD
    scale = head_dim ** (-0.5)
    positions = (block_order[:, None] * TOK_DEV + jnp.arange(TOK_DEV, dtype=jnp.int32)[None, :]).reshape(-1).astype(jnp.int32)

    def heads_first(x, turned):
        y = x.reshape(seq_len, heads, head_dim)
        if turned:
            y = rotate(y.astype(jnp.float32), positions, head_dim // 2).astype(jnp.bfloat16)
        return jnp.transpose(y, (1, 0, 2))

    def one_sample(items):
        query_s, key_s, value_s, tquery_s, tkey_s, tvalue_s, ids_s, cot_s = items
        same_clip = ids_s[:, None] == ids_s[None, :]

        def one_head(head_items):
            qh, kh, vh, tqh, tkh, tvh = head_items
            scores = jnp.dot(qh, kh.T, preferred_element_type=jnp.float32) * scale
            scores = jnp.where(same_clip, scores, -jnp.inf)
            slopes = (jnp.dot(tqh, kh.T, preferred_element_type=jnp.float32) + jnp.dot(qh, tkh.T, preferred_element_type=jnp.float32)) * scale
            best = lax.optimization_barrier(jnp.max(scores, axis=1, keepdims=True))
            weights = jnp.exp(scores - best)
            tilted = weights * slopes
            total = lax.optimization_barrier(jnp.sum(weights, axis=1, keepdims=True))
            weighted = lax.optimization_barrier(jnp.sum(tilted, axis=1, keepdims=True))
            weights_b = weights.astype(jnp.bfloat16)
            tilted_b = tilted.astype(jnp.bfloat16)
            primal = jnp.dot(weights_b, vh, preferred_element_type=jnp.float32)
            slope_part = jnp.dot(tilted_b, vh, preferred_element_type=jnp.float32)
            spread = jnp.dot(weights_b, tvh, preferred_element_type=jnp.float32)
            mean_out = primal / total
            return ((slope_part + spread) / total - weighted / total * mean_out).astype(jnp.bfloat16)
        head_outs = lax.map(one_head, (heads_first(query_s, True), heads_first(key_s, True), heads_first(value_s, False), heads_first(tquery_s, True), heads_first(tkey_s, True), heads_first(tvalue_s, False)))
        rows = jnp.transpose(head_outs, (1, 0, 2)).reshape(seq_len, heads * head_dim)
        projected = jnp.dot(rows, out_weight, preferred_element_type=jnp.float32)
        branch = (layer_scale * projected).astype(jnp.bfloat16)
        return (branch, lax.optimization_barrier(jnp.sum(cot_s.astype(jnp.float32) * projected, axis=0)))
    branch, partial_grad = lax.map(one_sample, (queries, keys, values, tangent_queries, tangent_keys, tangent_values, clip_ids, cotangent))
    return (branch, lax.optimization_barrier(jnp.sum(partial_grad, axis=0)) / math.sqrt(SAMPLES * seq_len))
```

```python
import functools
import math

import jax
import jax.numpy as jnp
from jax import lax
from jax.experimental import pallas as pl
from jax.experimental.pallas import tpu as pltpu
from jax.sharding import PartitionSpec as P

HEADS = 12
ID_ROWS = 16
MASK = -3e38
MIB = 2**20


def frequencies(lane, half):
    index = lane % half
    low = 1 << (half.bit_length() // 2)

    def pick(part, count, step):
        factor = jnp.ones(lane.shape, jnp.float32)
        for k in range(1, count):
            factor = jnp.where(part == k, 10000.0 ** (-k * step / half), factor)
        return factor

    return pick(index // low, half // low, low) * pick(index % low, low, 1)


def rotation(order_ref, rows, head_dim):
    half = head_dim // 2
    lane = lax.broadcasted_iota(jnp.int32, (8, head_dim), 1)
    line = lax.broadcasted_iota(jnp.int32, (8, head_dim), 0)
    frequency = frequencies(lane, half)
    base = order_ref[lax.axis_index("ctx")] * rows
    steps = rows // 8
    angles = jnp.concatenate(
        [line.astype(jnp.float32) * frequency]
        + [(base + 8 * (line + 8 * k)).astype(jnp.float32) * frequency for k in range(steps // 8)],
        axis=0,
    )
    cosines, sines = jnp.cos(angles), jnp.sin(angles)
    cos_v, sin_v = cosines[:8], sines[:8]
    cos_rows, sin_rows = [], []
    for u in range(steps):
        cos_u, sin_u = cosines[8 + u : 9 + u], sines[8 + u : 9 + u]
        cos_rows.append(cos_u * cos_v - sin_u * sin_v)
        sin_rows.append(jnp.where(lane < half, -1.0, 1.0) * (sin_u * cos_v + cos_u * sin_v))
    return jnp.concatenate(cos_rows, axis=0), jnp.concatenate(sin_rows, axis=0)


def group_of(offsets, members):
    me = lax.axis_index("ctx")
    even, odd = offsets
    offset = even if even == odd else jnp.where(me % members % 2 == 0, even, odd)
    return (me // members) ^ offset


def pack_kernel(route, members, turns, with_ids, order_hbm, ids_hbm, *refs):
    n_in = 2 * len(turns)
    sources, outs, (scratch, in_sems, order_ref, ids_ref, small_sems) = refs[:n_in], refs[n_in:-5], refs[-5:]
    loads = [pltpu.make_async_copy(order_hbm, order_ref, small_sems.at[0]), pltpu.make_async_copy(ids_hbm, ids_ref, small_sems.at[1])]
    loads += [pltpu.make_async_copy(source.at[0], scratch.at[t], in_sems.at[t]) for t, source in enumerate(sources)]
    for load in loads:
        load.start()
    rows, features = scratch.shape[1:]
    per_group = HEADS // len(route)
    head_dim = features // HEADS
    places = [group_of(offsets, members) for offsets in route]
    loads[0].wait()
    cosine, sine = rotation(order_ref, rows, head_dim)

    def turned(x):
        x = x.astype(jnp.float32)
        return (x * cosine + pltpu.roll(x, head_dim // 2, 1) * sine).astype(jnp.bfloat16)

    loads[1].wait()
    if with_ids:
        ids = jnp.broadcast_to(ids_ref[...].astype(jnp.float32), (ID_ROWS, rows)).astype(jnp.bfloat16)
        for out in outs:
            out[per_group * len(turns) * rows :, :head_dim] = ids
            out[per_group * len(turns) * rows :, head_dim:] = ids
    for t in range(n_in):
        loads[2 + t].wait()
        for group, out in zip(places, outs):
            for i in range(per_group):
                column = pl.multiple_of((group * per_group + i) * head_dim, head_dim)
                x = scratch[t, :, pl.ds(column, head_dim)]
                at = (i * len(turns) + t // 2) * rows
                out[at : at + rows, t % 2 * head_dim : (t % 2 + 1) * head_dim] = turned(x) if turns[t // 2] else x


def arrived_kernel(*refs):
    refs[-1][...] = jnp.zeros(refs[-1].shape, refs[-1].dtype)


def stage_kernel(w_hbm, cot_hbm, after_ref, w_ref, cot_ref, done_ref, sems):
    copies = [pltpu.make_async_copy(w_hbm, w_ref, sems.at[0]), pltpu.make_async_copy(cot_hbm, cot_ref, sems.at[1])]
    for copy in copies:
        copy.start()
    done_ref[...] = jnp.zeros(done_ref.shape, done_ref.dtype)
    for copy in copies:
        copy.wait()


def merge_kernel(*refs):
    packs, (out, features) = refs[:-3], refs[-2:]
    places = len(packs)
    size, both = packs[0].shape
    head_dim = both // 2
    rows, keep = head_dim, size - ID_ROWS
    lane = lax.broadcasted_iota(jnp.int32, (rows, head_dim), 1).astype(jnp.float32)
    for p, pack in enumerate(packs):
        out[p * keep : (p + 1) * keep, :] = pack[:keep, :]
        ids = pack[keep:, :head_dim].astype(jnp.float32)[0:1]
        hit = jnp.transpose(jnp.broadcast_to(ids, (head_dim, rows))) == lane
        other = jnp.where(hit, 0.0, MASK).astype(jnp.bfloat16)
        features[p * rows : (p + 1) * rows, :head_dim] = other
        features[p * rows : (p + 1) * rows, head_dim:] = jnp.where(hit, 1.0, 0.0).astype(jnp.bfloat16)
        at = places * keep + p // 2 * rows
        out[at : at + rows, p % 2 * head_dim : (p % 2 + 1) * head_dim] = other


def attend_kernel(groups, members, places, scale, *refs):
    half = groups // 2
    packs, features, merged, refs = refs[:groups], refs[groups : groups + 2], refs[groups + 2 : groups + 2 * members], refs[groups + 2 * members :]
    queries, outs = refs[: len(places)], refs[-len(places) :]
    rows, part = outs[0].shape
    size, both = packs[0].shape
    head_dim = both // 2
    keep = size - ID_ROWS
    nt = (((1,), (1,)), ((), ()))
    blocks = [(pack, 0) for pack in packs] + [(other, p * keep) for other in merged for p in range(half)]
    other_clip = [(ref, p * rows, 0) for ref in features for p in range(half)]
    other_clip += [(other, half * keep + p // 2 * rows, p % 2 * head_dim) for other in merged for p in range(half)]
    same = jnp.concatenate([features[p // half][p % half * rows : (p % half + 1) * rows, head_dim:] for p in places], axis=0)

    def products(i):
        q = jnp.concatenate([query[i * rows : (i + 1) * rows, :] for query in queries], axis=0)
        q_masked = jnp.concatenate([q[:, head_dim:], same], axis=1)
        scores, slopes = [], []
        for b in range(0, len(blocks), 2):
            pair = [(ref, at + 2 * i * rows) for ref, at in blocks[b : b + 2]]
            masks = [ref[at : at + rows, col : col + head_dim] for ref, at, col in other_clip[b : b + 2]]
            keys = jnp.concatenate([ref[at : at + rows, :] for ref, at in pair], axis=0)
            masked = [jnp.concatenate([ref[at : at + rows, :head_dim], mask], axis=1) for (ref, at), mask in zip(pair, masks)]
            scores.append(lax.dot_general(q_masked, jnp.concatenate(masked, axis=0), nt, preferred_element_type=jnp.float32))
            slopes.append(lax.dot_general(q, keys, nt, preferred_element_type=jnp.float32))
        return scores, slopes

    def finish(i, scores, slopes):
        best = functools.reduce(jnp.maximum, scores)
        best = jnp.max(best, axis=1, keepdims=True)
        weights = [jnp.exp2((score - best) * (scale * math.log2(math.e))) for score in scores]
        tilted = [weight * slope for weight, slope in zip(weights, slopes)]
        total = 1.0 / jnp.sum(functools.reduce(lambda a, b: a + b, weights), axis=1, keepdims=True)
        weights = jnp.concatenate([weight.astype(jnp.bfloat16) for weight in weights], axis=1)
        tilted = jnp.concatenate([tilt.astype(jnp.bfloat16) for tilt in tilted], axis=1)
        vals = jnp.concatenate([ref[at + (2 * i + 1) * rows : at + (2 * i + 2) * rows, :] for ref, at in blocks], axis=0)
        ones = jnp.ones((vals.shape[0], head_dim), jnp.bfloat16)
        mixed = jnp.dot(weights, vals, preferred_element_type=jnp.float32)
        leaned = jnp.dot(tilted, jnp.concatenate([vals[:, :head_dim], ones], axis=1), preferred_element_type=jnp.float32)
        primal, spread = mixed[:, :head_dim], mixed[:, head_dim:]
        slope_part, weighted = leaned[:, :head_dim], leaned[:, head_dim:]
        out = ((slope_part - weighted * (primal * total)) * scale + spread) * total
        for k, ref in enumerate(outs):
            ref[:, i * head_dim : (i + 1) * head_dim] = out[k * rows : (k + 1) * rows].astype(jnp.bfloat16)

    ready = products(0)
    for i in range(part // head_dim):
        following = products(i + 1) if (i + 1) * head_dim < part else None
        finish(i, *ready)
        ready = following


def part_kernel(members, offsets, tile, ta_ref, w_ref, *refs):
    begun, out_ref = refs[:-1], refs[-1]
    group = group_of(offsets, members)
    width = ta_ref.shape[1]
    place = pl.ds(pl.multiple_of(group * width, width), width)
    for j in range(w_ref.shape[1] // tile):
        cols = slice(j * tile, (j + 1) * tile)
        part = jnp.dot(ta_ref[...], w_ref[place, cols], preferred_element_type=jnp.float32)
        out_ref[:, cols] = begun[0][:, cols] + part if begun else part


def project_kernel(members, offsets, tile, ta_ref, w_ref, begun_ref, cot_ref, projected_ref, grad_ref):
    group = group_of(offsets, members)
    width = ta_ref.shape[1]
    place = pl.ds(pl.multiple_of(group * width, width), width)
    for j in range(w_ref.shape[1] // tile):
        cols = slice(j * tile, (j + 1) * tile)
        projected = begun_ref[:, cols] + jnp.dot(ta_ref[...], w_ref[place, cols], preferred_element_type=jnp.float32)
        projected_ref[:, cols] = projected
        grad_ref[:, cols] = jnp.sum(cot_ref[0, :, cols].astype(jnp.float32) * projected, axis=0, keepdims=True)


def branch_kernel(projected_ref, scale_ref, branch_ref):
    branch_ref[0] = (scale_ref[...] * projected_ref[...]).astype(jnp.bfloat16)


def sum_kernel(factor, *refs):
    terms = [ref[...] for ref in refs[:-1]]
    while len(terms) > 1:
        terms = [terms[i] + terms[i + 1] for i in range(0, len(terms), 2)]
    refs[-1][...] = terms[0] * factor


def exchange_sum(x, partners, factor=1.0):
    n_ctx, n_dp = lax.axis_size("ctx"), lax.axis_size("dp")
    places = [(j, z) for j in range(n_ctx) for z in range(n_dp)]
    terms = [lax.ppermute(x, ("ctx", "dp"), [(j * n_dp + z, (j ^ own) * n_dp + (z ^ other)) for j, z in places]) for own, other in partners]
    return pl.pallas_call(
        functools.partial(sum_kernel, factor),
        out_shape=jax.ShapeDtypeStruct(x.shape, x.dtype),
        compiler_params=pltpu.CompilerParams(vmem_limit_bytes=16 * MIB),
        name="sum",
    )(*terms, x)


def local(queries, keys, values, tangent_queries, tangent_keys, tangent_values, clip_ids, block_order, out_weight, layer_scale, cotangent):
    n_ctx, n_dp = lax.axis_size("ctx"), lax.axis_size("dp")
    rows, features = queries.shape[1:]
    head_dim = features // HEADS
    width = out_weight.shape[1]
    groups = math.gcd(n_ctx, HEADS)
    members = n_ctx // groups
    per_group = HEADS // groups
    vmem = pl.BlockSpec(memory_space=pltpu.VMEM)
    hbm = pl.BlockSpec(memory_space=pltpu.HBM)
    bf16 = jnp.bfloat16

    cross = 1 if members > 1 else 0

    def swap(x, offset):
        return lax.ppermute(x, "ctx", [(j, j ^ offset) for j in range(n_ctx)])

    far = sorted((offset for offset in range(groups) if offset.bit_count() > 1), key=lambda offset: -offset.bit_count())
    near = [offset for offset in range(groups) if offset.bit_count() == 1]
    route = [(0, 0)] + [(offset, offset) for offset in far] + list(zip(near, reversed(near)))
    early, late = [*range(1 + len(far))], [*range(1 + len(far), groups)]

    def send(x, place):
        return lax.ppermute(x, "ctx", [(j, j ^ (route[place][j % members % 2] * members + cross)) for j in range(n_ctx)])

    def send_back(x, place):
        return lax.ppermute(x, "ctx", [(j ^ (route[place][j % members % 2] * members + cross), j) for j in range(n_ctx)])

    kv_pack = (2 * per_group * rows + ID_ROWS, 2 * head_dim)
    q_pack = (per_group * rows, 2 * head_dim)

    def in_hbm(x):
        return pltpu.with_memory_space_constraint(x, pltpu.HBM)

    def pack(name, shape, turns, with_ids, sources):
        return pl.pallas_call(
            functools.partial(pack_kernel, route, members, turns, with_ids),
            out_shape=[pltpu.VMEM(shape, bf16)] * groups,
            in_specs=[hbm] * (2 + len(sources)),
            out_specs=[vmem] * groups,
            scratch_shapes=[
                pltpu.VMEM((len(sources), rows, features), bf16),
                pltpu.SemaphoreType.DMA((len(sources),)),
                pltpu.SMEM(block_order.shape, jnp.int32),
                pltpu.VMEM(clip_ids.shape, jnp.int32),
                pltpu.SemaphoreType.DMA((2,)),
            ],
            compiler_params=pltpu.CompilerParams(vmem_limit_bytes=16 * MIB),
            name=name,
        )(*map(in_hbm, (block_order, clip_ids) + sources))

    kv = pack("pack_keys", kv_pack, (True, False), True, (keys, tangent_keys, values, tangent_values))
    q = list(pack("pack_queries", q_pack, (True,), False, (tangent_queries, queries)))
    weight, cot, staged = pl.pallas_call(
        stage_kernel,
        out_shape=[pltpu.VMEM(out_weight.shape, bf16), pltpu.VMEM(cotangent.shape, bf16), pltpu.VMEM((8, 128), jnp.float32)],
        in_specs=[hbm, hbm, vmem],
        out_specs=[vmem] * 3,
        scratch_shapes=[pltpu.SemaphoreType.DMA((2,))],
        compiler_params=pltpu.CompilerParams(vmem_limit_bytes=16 * MIB),
        name="stage",
    )(in_hbm(out_weight), in_hbm(cotangent), q[0])

    def exchange(sent):
        return [sent[0]] + [send(sent[place], place) for place in range(1, groups)]

    kv = exchange(kv)
    q = exchange(q)

    def merge(name, packs, after):
        places = len(packs)
        return pl.pallas_call(
            merge_kernel,
            out_shape=[
                jax.ShapeDtypeStruct((places * 2 * per_group * rows + places // 2 * rows, 2 * head_dim), bf16),
                jax.ShapeDtypeStruct((places * rows, 2 * head_dim), bf16),
            ],
            in_specs=[vmem] * (places + 1),
            out_specs=[vmem] * 2,
            compiler_params=pltpu.CompilerParams(vmem_limit_bytes=16 * MIB),
            name=name,
        )(*packs, after)

    merged_first, features_first = merge("merge_first", kv[: groups // 2], q[0])
    merged_last, features_last = merge("merge_last", kv[groups // 2 :], staged)
    others = [swap(merged, s) for s in range(1, members) for merged in (merged_first, merged_last)]
    arrived = pl.pallas_call(
        arrived_kernel,
        out_shape=jax.ShapeDtypeStruct((8, 128), jnp.float32),
        in_specs=[vmem] * len(early),
        out_specs=vmem,
        compiler_params=pltpu.CompilerParams(vmem_limit_bytes=16 * MIB),
        cost_estimate=pl.CostEstimate(flops=10**11, bytes_accessed=MIB, transcendentals=0),
        name="arrived",
    )(*(q[place] for place in early))

    def attend(name, places, *after):
        return pl.pallas_call(
            functools.partial(attend_kernel, groups, members, places, head_dim ** (-0.5)),
            out_shape=[jax.ShapeDtypeStruct((rows, per_group * head_dim), bf16)] * len(places),
            in_specs=[vmem] * (groups + 2 * members + len(places) + len(after)),
            out_specs=[vmem] * len(places),
            compiler_params=pltpu.CompilerParams(vmem_limit_bytes=24 * MIB),
            name=name,
        )(*kv, features_first, features_last, *others, *(q[place] for place in places), *after)

    done = dict(zip(early, attend("attend_early", early, arrived)))
    for place in early[1:]:
        done[place] = send_back(done[place], place)
    done.update(zip(late, attend("attend_late", late)))
    for place in late:
        done[place] = send_back(done[place], place)
    arrivals = [*early, *late]
    begun = None
    for place in arrivals[:-1]:
        begun = pl.pallas_call(
            functools.partial(part_kernel, members, route[place], 512),
            out_shape=jax.ShapeDtypeStruct((rows, width), jnp.float32),
            in_specs=[vmem] * (2 + (begun is not None)),
            out_specs=vmem,
            compiler_params=pltpu.CompilerParams(vmem_limit_bytes=16 * MIB),
            name=f"part{place}",
        )(done[place], weight, *([] if begun is None else [begun]))
    projected, grad = pl.pallas_call(
        functools.partial(project_kernel, members, route[arrivals[-1]], 512),
        out_shape=[jax.ShapeDtypeStruct((rows, width), jnp.float32), jax.ShapeDtypeStruct((1, width), jnp.float32)],
        in_specs=[vmem] * 4,
        out_specs=[vmem] * 2,
        compiler_params=pltpu.CompilerParams(vmem_limit_bytes=16 * MIB),
        name="project",
    )(done[arrivals[-1]], weight, begun, cot)
    branch = pl.pallas_call(
        branch_kernel,
        out_shape=jax.ShapeDtypeStruct((1, rows, width), bf16),
        in_specs=[vmem] * 2,
        out_specs=vmem,
        compiler_params=pltpu.CompilerParams(vmem_limit_bytes=16 * MIB),
        name="branch",
    )(projected, layer_scale[None, :])
    summed = exchange_sum(grad, [(s, 0) for s in reversed(range(1, members))])
    summed = exchange_sum(summed, [(offset + cross, 0) for offset in reversed(range(members, n_ctx, members))])
    factor = 1.0 / math.sqrt(n_ctx * n_dp * rows)
    offsets = [1 << k for k in range(n_dp.bit_length() - 1)]
    for offset in offsets:
        summed = exchange_sum(summed, [(cross, offset)], factor if offset == offsets[-1] else 1.0)
    return branch, summed[0]


def solution(mesh):
    tokens = P("dp", "ctx", None)
    in_specs = (tokens,) * 6 + (P("dp", "ctx"), P(), P(), P(), tokens)
    return jax.shard_map(local, mesh=mesh, in_specs=in_specs, out_specs=(tokens, P()), check_vma=False)
```

```python
import functools
import math

import jax
import jax.numpy as jnp
from jax import lax
from jax.experimental import pallas as pl
from jax.experimental.pallas import tpu as pltpu
from jax.sharding import PartitionSpec as P

HEADS = 12
ID_ROWS = 16
MASK = -3e38
MIB = 2**20


def frequencies(lane, half):
    index = lane % half
    low = 1 << (half.bit_length() // 2)

    def pick(part, count, step):
        factor = jnp.ones(lane.shape, jnp.float32)
        for k in range(1, count):
            factor = jnp.where(part == k, 10000.0 ** (-k * step / half), factor)
        return factor

    return pick(index // low, half // low, low) * pick(index % low, low, 1)


def rotation(order_ref, rows, head_dim):
    half = head_dim // 2
    lane = lax.broadcasted_iota(jnp.int32, (8, head_dim), 1)
    line = lax.broadcasted_iota(jnp.int32, (8, head_dim), 0)
    frequency = frequencies(lane, half)
    base = order_ref[lax.axis_index("ctx")] * rows
    steps = rows // 8
    angles = jnp.concatenate(
        [line.astype(jnp.float32) * frequency]
        + [(base + 8 * (line + 8 * k)).astype(jnp.float32) * frequency for k in range(steps // 8)],
        axis=0,
    )
    cosines, sines = jnp.cos(angles), jnp.sin(angles)
    cos_v, sin_v = cosines[:8], sines[:8]
    cos_rows, sin_rows = [], []
    for u in range(steps):
        cos_u, sin_u = cosines[8 + u : 9 + u], sines[8 + u : 9 + u]
        cos_rows.append(cos_u * cos_v - sin_u * sin_v)
        sin_rows.append(jnp.where(lane < half, -1.0, 1.0) * (sin_u * cos_v + cos_u * sin_v))
    return jnp.concatenate(cos_rows, axis=0), jnp.concatenate(sin_rows, axis=0)


def odd_one(group, place):
    bits = group
    for shift in (4, 2, 1):
        bits = bits ^ (bits >> shift)
    return ((bits & 1) + place) % 2


def group_of(offsets, members):
    me = lax.axis_index("ctx")
    group = me // members
    even, odd = offsets
    return group ^ (even if even == odd else jnp.where(odd_one(group, me % members) == 0, even, odd))


def pack_kernel(offsets, members, turns, with_ids, order_hbm, ids_hbm, *refs):
    n_in = 2 * len(turns)
    sources, outs, (scratch, in_sems, order_ref, ids_ref, small_sems) = refs[:n_in], refs[n_in:-5], refs[-5:]
    rows, part = scratch.shape[2:]
    head_dim = outs[0].shape[1] // 2
    per_group = part // head_dim
    small = [pltpu.make_async_copy(order_hbm, order_ref, small_sems.at[0]), pltpu.make_async_copy(ids_hbm, ids_ref, small_sems.at[1])]
    for load in small:
        load.start()
    loads = {}
    for t, source in enumerate(sources):
        for p, pair in enumerate(offsets):
            column = pl.multiple_of(group_of(pair, members) * part, part)
            loads[t, p] = pltpu.make_async_copy(source.at[0, :, pl.ds(column, part)], scratch.at[t, p], in_sems.at[t, p])
            loads[t, p].start()
    small[0].wait()
    cosine, sine = rotation(order_ref, rows, head_dim)

    def turned(x):
        x = x.astype(jnp.float32)
        return (x * cosine + pltpu.roll(x, head_dim // 2, 1) * sine).astype(jnp.bfloat16)

    small[1].wait()
    if with_ids:
        ids = jnp.broadcast_to(ids_ref[...].astype(jnp.float32), (ID_ROWS, rows)).astype(jnp.bfloat16)
        for out in outs:
            out[per_group * len(turns) * rows :, :head_dim] = ids
            out[per_group * len(turns) * rows :, head_dim:] = ids
    for t in range(n_in):
        for p, out in enumerate(outs):
            loads[t, p].wait()
            for i in range(per_group):
                x = scratch[t, p, :, i * head_dim : (i + 1) * head_dim]
                at = (i * len(turns) + t // 2) * rows
                out[at : at + rows, t % 2 * head_dim : (t % 2 + 1) * head_dim] = turned(x) if turns[t // 2] else x


def arrived_kernel(*refs):
    refs[-1][...] = jnp.zeros(refs[-1].shape, refs[-1].dtype)


def stage_kernel(w_hbm, cot_hbm, after_ref, w_ref, cot_ref, done_ref, sems):
    copies = [pltpu.make_async_copy(w_hbm, w_ref, sems.at[0]), pltpu.make_async_copy(cot_hbm, cot_ref, sems.at[1])]
    for copy in copies:
        copy.start()
    done_ref[...] = jnp.zeros(done_ref.shape, done_ref.dtype)
    for copy in copies:
        copy.wait()


def merge_kernel(*refs):
    packs, (out, features) = refs[:-3], refs[-2:]
    places = len(packs)
    size, both = packs[0].shape
    head_dim = both // 2
    rows, keep = head_dim, size - ID_ROWS
    lane = lax.broadcasted_iota(jnp.int32, (rows, head_dim), 1).astype(jnp.float32)
    for p, pack in enumerate(packs):
        out[p * keep : (p + 1) * keep, :] = pack[:keep, :]
        ids = pack[keep:, :head_dim].astype(jnp.float32)[0:1]
        hit = jnp.transpose(jnp.broadcast_to(ids, (head_dim, rows))) == lane
        other = jnp.where(hit, 0.0, MASK).astype(jnp.bfloat16)
        features[p * rows : (p + 1) * rows, :head_dim] = other
        features[p * rows : (p + 1) * rows, head_dim:] = jnp.where(hit, 1.0, 0.0).astype(jnp.bfloat16)
        at = places * keep + p // 2 * rows
        out[at : at + rows, p % 2 * head_dim : (p % 2 + 1) * head_dim] = other


def attend_kernel(groups, members, places, scale, *refs):
    half = groups // 2
    packs, features, merged, refs = refs[:groups], refs[groups : groups + 2], refs[groups + 2 : groups + 2 * members], refs[groups + 2 * members :]
    queries, outs = refs[: len(places)], refs[-len(places) :]
    rows, part = outs[0].shape
    size, both = packs[0].shape
    head_dim = both // 2
    keep = size - ID_ROWS
    nt = (((1,), (1,)), ((), ()))
    blocks = [(pack, 0) for pack in packs] + [(other, p * keep) for other in merged for p in range(half)]
    other_clip = [(ref, p * rows, 0) for ref in features for p in range(half)]
    other_clip += [(other, half * keep + p // 2 * rows, p % 2 * head_dim) for other in merged for p in range(half)]
    same = jnp.concatenate([features[p // half][p % half * rows : (p % half + 1) * rows, head_dim:] for p in places], axis=0)

    def products(i):
        q = jnp.concatenate([query[i * rows : (i + 1) * rows, :] for query in queries], axis=0)
        q_masked = jnp.concatenate([q[:, head_dim:], same], axis=1)
        scores, slopes = [], []
        for b in range(0, len(blocks), 2):
            pair = [(ref, at + 2 * i * rows) for ref, at in blocks[b : b + 2]]
            masks = [ref[at : at + rows, col : col + head_dim] for ref, at, col in other_clip[b : b + 2]]
            keys = jnp.concatenate([ref[at : at + rows, :] for ref, at in pair], axis=0)
            masked = [jnp.concatenate([ref[at : at + rows, :head_dim], mask], axis=1) for (ref, at), mask in zip(pair, masks)]
            scores.append(lax.dot_general(q_masked, jnp.concatenate(masked, axis=0), nt, preferred_element_type=jnp.float32))
            slopes.append(lax.dot_general(q, keys, nt, preferred_element_type=jnp.float32))
        return scores, slopes

    def finish(i, scores, slopes):
        best = functools.reduce(jnp.maximum, scores)
        best = jnp.max(best, axis=1, keepdims=True)
        weights = [jnp.exp2((score - best) * (scale * math.log2(math.e))) for score in scores]
        tilted = [weight * slope for weight, slope in zip(weights, slopes)]
        total = 1.0 / jnp.sum(functools.reduce(lambda a, b: a + b, weights), axis=1, keepdims=True)
        weights = jnp.concatenate([weight.astype(jnp.bfloat16) for weight in weights], axis=1)
        tilted = jnp.concatenate([tilt.astype(jnp.bfloat16) for tilt in tilted], axis=1)
        vals = jnp.concatenate([ref[at + (2 * i + 1) * rows : at + (2 * i + 2) * rows, :] for ref, at in blocks], axis=0)
        ones = jnp.ones((vals.shape[0], head_dim), jnp.bfloat16)
        mixed = jnp.dot(weights, vals, preferred_element_type=jnp.float32)
        leaned = jnp.dot(tilted, jnp.concatenate([vals[:, :head_dim], ones], axis=1), preferred_element_type=jnp.float32)
        primal, spread = mixed[:, :head_dim], mixed[:, head_dim:]
        slope_part, weighted = leaned[:, :head_dim], leaned[:, head_dim:]
        out = ((slope_part - weighted * (primal * total)) * scale + spread) * total
        for k, ref in enumerate(outs):
            ref[:, i * head_dim : (i + 1) * head_dim] = out[k * rows : (k + 1) * rows].astype(jnp.bfloat16)

    ready = products(0)
    for i in range(part // head_dim):
        following = products(i + 1) if (i + 1) * head_dim < part else None
        finish(i, *ready)
        ready = following


def part_kernel(members, offsets, tile, ta_ref, w_ref, *refs):
    begun, out_ref = refs[:-1], refs[-1]
    group = group_of(offsets, members)
    width = ta_ref.shape[1]
    place = pl.ds(pl.multiple_of(group * width, width), width)
    for j in range(w_ref.shape[1] // tile):
        cols = slice(j * tile, (j + 1) * tile)
        part = jnp.dot(ta_ref[...], w_ref[place, cols], preferred_element_type=jnp.float32)
        out_ref[:, cols] = begun[0][:, cols] + part if begun else part


def project_kernel(members, offsets, tile, ta_ref, w_ref, begun_ref, cot_ref, projected_ref, grad_ref):
    group = group_of(offsets, members)
    width = ta_ref.shape[1]
    place = pl.ds(pl.multiple_of(group * width, width), width)
    for j in range(w_ref.shape[1] // tile):
        cols = slice(j * tile, (j + 1) * tile)
        projected = begun_ref[:, cols] + jnp.dot(ta_ref[...], w_ref[place, cols], preferred_element_type=jnp.float32)
        projected_ref[:, cols] = projected
        grad_ref[:, cols] = jnp.sum(cot_ref[0, :, cols].astype(jnp.float32) * projected, axis=0, keepdims=True)


def branch_kernel(projected_ref, scale_ref, branch_ref):
    branch_ref[0] = (scale_ref[...] * projected_ref[...]).astype(jnp.bfloat16)


def sum_kernel(factor, *refs):
    terms = [ref[...] for ref in refs[:-1]]
    while len(terms) > 1:
        terms = [terms[i] + terms[i + 1] for i in range(0, len(terms), 2)]
    refs[-1][...] = terms[0] * factor


def exchange_sum(x, partners, factor=1.0):
    n_ctx, n_dp = lax.axis_size("ctx"), lax.axis_size("dp")
    places = [(j, z) for j in range(n_ctx) for z in range(n_dp)]
    terms = [lax.ppermute(x, ("ctx", "dp"), [(j * n_dp + z, (j ^ own) * n_dp + (z ^ other)) for j, z in places]) for own, other in partners]
    return pl.pallas_call(
        functools.partial(sum_kernel, factor),
        out_shape=jax.ShapeDtypeStruct(x.shape, x.dtype),
        compiler_params=pltpu.CompilerParams(vmem_limit_bytes=16 * MIB),
        name="sum",
    )(*terms, x)


def local(queries, keys, values, tangent_queries, tangent_keys, tangent_values, clip_ids, block_order, out_weight, layer_scale, cotangent):
    n_ctx, n_dp = lax.axis_size("ctx"), lax.axis_size("dp")
    rows, features = queries.shape[1:]
    head_dim = features // HEADS
    width = out_weight.shape[1]
    groups = math.gcd(n_ctx, HEADS)
    members = n_ctx // groups
    per_group = HEADS // groups
    vmem = pl.BlockSpec(memory_space=pltpu.VMEM)
    hbm = pl.BlockSpec(memory_space=pltpu.HBM)
    bf16 = jnp.bfloat16

    cross = 1 if members > 1 else 0

    def swap(x, offset):
        return lax.ppermute(x, "ctx", [(j, j ^ offset) for j in range(n_ctx)])

    far = sorted((offset for offset in range(groups) if offset.bit_count() > 1), key=lambda offset: -offset.bit_count())
    near = [offset for offset in range(groups) if offset.bit_count() == 1]
    route = [(0, 0)] + [(offset, offset) for offset in far] + list(zip(near, reversed(near)))
    early, late = [*range(1 + len(far))], [*range(1 + len(far), groups)]

    def send(x, place):
        offset = [route[place][odd_one(j // members, j % members)] for j in range(n_ctx)]
        return lax.ppermute(x, "ctx", [(j, j ^ (offset[j] * members + cross)) for j in range(n_ctx)])

    kv_pack = (2 * per_group * rows + ID_ROWS, 2 * head_dim)
    q_pack = (per_group * rows, 2 * head_dim)

    def in_hbm(x):
        return pltpu.with_memory_space_constraint(x, pltpu.HBM)

    def pack(name, places, shape, turns, with_ids, sources):
        return pl.pallas_call(
            functools.partial(pack_kernel, [route[place] for place in places], members, turns, with_ids),
            out_shape=[pltpu.VMEM(shape, bf16)] * len(places),
            in_specs=[hbm] * (2 + len(sources)),
            out_specs=[vmem] * len(places),
            scratch_shapes=[
                pltpu.VMEM((len(sources), len(places), rows, per_group * head_dim), bf16),
                pltpu.SemaphoreType.DMA((len(sources), len(places))),
                pltpu.SMEM(block_order.shape, jnp.int32),
                pltpu.VMEM(clip_ids.shape, jnp.int32),
                pltpu.SemaphoreType.DMA((2,)),
            ],
            compiler_params=pltpu.CompilerParams(vmem_limit_bytes=16 * MIB),
            name=name,
        )(*map(in_hbm, (block_order, clip_ids) + sources))

    key_sources = (keys, tangent_keys, values, tangent_values)
    far_kv = pack("pack_far", early[1:], kv_pack, (True, False), True, key_sources)
    near_kv = pack("pack_near", [0, *late], kv_pack, (True, False), True, key_sources)
    kv = [near_kv[0], *far_kv, *near_kv[1:]]
    q = list(pack("pack_queries", range(groups), q_pack, (True,), False, (tangent_queries, queries)))

    weight, cot, staged = pl.pallas_call(
        stage_kernel,
        out_shape=[pltpu.VMEM(out_weight.shape, bf16), pltpu.VMEM(cotangent.shape, bf16), pltpu.VMEM((8, 128), jnp.float32)],
        in_specs=[hbm, hbm, vmem],
        out_specs=[vmem] * 3,
        scratch_shapes=[pltpu.SemaphoreType.DMA((2,))],
        compiler_params=pltpu.CompilerParams(vmem_limit_bytes=16 * MIB),
        name="stage",
    )(in_hbm(out_weight), in_hbm(cotangent), q[0])

    def exchange(sent):
        return [sent[0]] + [send(sent[place], place) for place in range(1, groups)]

    kv = exchange(kv)
    q = exchange(q)

    def merge(name, packs, after):
        places = len(packs)
        return pl.pallas_call(
            merge_kernel,
            out_shape=[
                jax.ShapeDtypeStruct((places * 2 * per_group * rows + places // 2 * rows, 2 * head_dim), bf16),
                jax.ShapeDtypeStruct((places * rows, 2 * head_dim), bf16),
            ],
            in_specs=[vmem] * (places + 1),
            out_specs=[vmem] * 2,
            compiler_params=pltpu.CompilerParams(vmem_limit_bytes=16 * MIB),
            name=name,
        )(*packs, after)

    merged_first, features_first = merge("merge_first", kv[: groups // 2], q[0])
    merged_last, features_last = merge("merge_last", kv[groups // 2 :], staged)
    others = [swap(merged, s) for s in range(1, members) for merged in (merged_first, merged_last)]
    arrived = pl.pallas_call(
        arrived_kernel,
        out_shape=jax.ShapeDtypeStruct((8, 128), jnp.float32),
        in_specs=[vmem] * len(early),
        out_specs=vmem,
        compiler_params=pltpu.CompilerParams(vmem_limit_bytes=16 * MIB),
        cost_estimate=pl.CostEstimate(flops=10**11, bytes_accessed=MIB, transcendentals=0),
        name="arrived",
    )(*(q[place] for place in early))

    def attend(name, places, *after):
        return pl.pallas_call(
            functools.partial(attend_kernel, groups, members, places, head_dim ** (-0.5)),
            out_shape=[jax.ShapeDtypeStruct((rows, per_group * head_dim), bf16)] * len(places),
            in_specs=[vmem] * (groups + 2 * members + len(places) + len(after)),
            out_specs=[vmem] * len(places),
            compiler_params=pltpu.CompilerParams(vmem_limit_bytes=24 * MIB),
            name=name,
        )(*kv, features_first, features_last, *others, *(q[place] for place in places), *after)

    done = dict(zip(early, attend("attend_early", early, arrived)))
    for place in early[1:]:
        done[place] = send(done[place], place)
    done.update(zip(late, attend("attend_late", late)))
    for place in late:
        done[place] = send(done[place], place)
    arrivals = [*early, *late]
    begun = None
    for place in arrivals[:-1]:
        begun = pl.pallas_call(
            functools.partial(part_kernel, members, route[place], 512),
            out_shape=jax.ShapeDtypeStruct((rows, width), jnp.float32),
            in_specs=[vmem] * (2 + (begun is not None)),
            out_specs=vmem,
            compiler_params=pltpu.CompilerParams(vmem_limit_bytes=16 * MIB),
            name=f"part{place}",
        )(done[place], weight, *([] if begun is None else [begun]))
    projected, grad = pl.pallas_call(
        functools.partial(project_kernel, members, route[arrivals[-1]], 512),
        out_shape=[jax.ShapeDtypeStruct((rows, width), jnp.float32), jax.ShapeDtypeStruct((1, width), jnp.float32)],
        in_specs=[vmem] * 4,
        out_specs=[vmem] * 2,
        compiler_params=pltpu.CompilerParams(vmem_limit_bytes=16 * MIB),
        name="project",
    )(done[arrivals[-1]], weight, begun, cot)
    branch = pl.pallas_call(
        branch_kernel,
        out_shape=jax.ShapeDtypeStruct((1, rows, width), bf16),
        in_specs=[vmem] * 2,
        out_specs=vmem,
        compiler_params=pltpu.CompilerParams(vmem_limit_bytes=16 * MIB),
        name="branch",
    )(projected, layer_scale[None, :])
    summed = exchange_sum(grad, [(s, 0) for s in reversed(range(1, members))])
    summed = exchange_sum(summed, [(offset + cross, 0) for offset in reversed(range(members, n_ctx, members))])
    summed = exchange_sum(summed, [(cross, offset) for offset in reversed(range(1, n_dp))], 1.0 / math.sqrt(n_ctx * n_dp * rows))
    return branch, summed[0]


def solution(mesh):
    tokens = P("dp", "ctx", None)
    in_specs = (tokens,) * 6 + (P("dp", "ctx"), P(), P(), P(), tokens)
    return jax.shard_map(local, mesh=mesh, in_specs=in_specs, out_specs=(tokens, P()), check_vma=False)
```

```python
import functools
import math

import jax
import jax.numpy as jnp
from jax import lax
from jax.experimental import pallas as pl
from jax.experimental.pallas import tpu as pltpu
from jax.sharding import PartitionSpec as P

HEADS = 12
ID_ROWS = 16
MASK = -3e38
MIB = 2**20


def frequencies(lane, half):
    index = lane % half
    low = 1 << (half.bit_length() // 2)

    def pick(part, count, step):
        factor = jnp.ones(lane.shape, jnp.float32)
        for k in range(1, count):
            factor = jnp.where(part == k, 10000.0 ** (-k * step / half), factor)
        return factor

    return pick(index // low, half // low, low) * pick(index % low, low, 1)


def rotation(order_ref, rows, head_dim):
    half = head_dim // 2
    lane = lax.broadcasted_iota(jnp.int32, (8, head_dim), 1)
    line = lax.broadcasted_iota(jnp.int32, (8, head_dim), 0)
    frequency = frequencies(lane, half)
    base = order_ref[lax.axis_index("ctx")] * rows
    steps = rows // 8
    angles = jnp.concatenate(
        [line.astype(jnp.float32) * frequency]
        + [(base + 8 * (line + 8 * k)).astype(jnp.float32) * frequency for k in range(steps // 8)],
        axis=0,
    )
    cosines, sines = jnp.cos(angles), jnp.sin(angles)
    cos_v, sin_v = cosines[:8], sines[:8]
    cos_rows, sin_rows = [], []
    for u in range(steps):
        cos_u, sin_u = cosines[8 + u : 9 + u], sines[8 + u : 9 + u]
        cos_rows.append(cos_u * cos_v - sin_u * sin_v)
        sin_rows.append(jnp.where(lane < half, -1.0, 1.0) * (sin_u * cos_v + cos_u * sin_v))
    return jnp.concatenate(cos_rows, axis=0), jnp.concatenate(sin_rows, axis=0)


def odd_one(group, place):
    bits = group
    for shift in (4, 2, 1):
        bits = bits ^ (bits >> shift)
    return ((bits & 1) + place) % 2


def group_of(offsets, members):
    me = lax.axis_index("ctx")
    group = me // members
    even, odd = offsets
    return group ^ (even if even == odd else jnp.where(odd_one(group, me % members) == 0, even, odd))


def pack_kernel(offsets, members, turns, with_ids, order_hbm, ids_hbm, *refs):
    n_in = 2 * len(turns)
    sources, outs, (scratch, in_sems, order_ref, ids_ref, small_sems) = refs[:n_in], refs[n_in:-5], refs[-5:]
    rows, part = scratch.shape[2:]
    head_dim = outs[0].shape[1] // 2
    per_group = part // head_dim
    small = [pltpu.make_async_copy(order_hbm, order_ref, small_sems.at[0]), pltpu.make_async_copy(ids_hbm, ids_ref, small_sems.at[1])]
    for load in small:
        load.start()
    loads = {}
    for t, source in enumerate(sources):
        for p, pair in enumerate(offsets):
            column = pl.multiple_of(group_of(pair, members) * part, part)
            loads[t, p] = pltpu.make_async_copy(source.at[0, :, pl.ds(column, part)], scratch.at[t, p], in_sems.at[t, p])
            loads[t, p].start()
    small[0].wait()
    cosine, sine = rotation(order_ref, rows, head_dim)

    def turned(x):
        x = x.astype(jnp.float32)
        return (x * cosine + pltpu.roll(x, head_dim // 2, 1) * sine).astype(jnp.bfloat16)

    small[1].wait()
    if with_ids:
        ids = jnp.broadcast_to(ids_ref[...].astype(jnp.float32), (ID_ROWS, rows)).astype(jnp.bfloat16)
        for out in outs:
            out[per_group * len(turns) * rows :, :head_dim] = ids
            out[per_group * len(turns) * rows :, head_dim:] = ids
    for t in range(n_in):
        for p, out in enumerate(outs):
            loads[t, p].wait()
            for i in range(per_group):
                x = scratch[t, p, :, i * head_dim : (i + 1) * head_dim]
                at = (i * len(turns) + t // 2) * rows
                out[at : at + rows, t % 2 * head_dim : (t % 2 + 1) * head_dim] = turned(x) if turns[t // 2] else x


def arrived_kernel(*refs):
    refs[-1][...] = jnp.zeros(refs[-1].shape, refs[-1].dtype)


def stage_kernel(w_hbm, cot_hbm, after_ref, w_ref, cot_ref, done_ref, sems):
    copies = [pltpu.make_async_copy(w_hbm, w_ref, sems.at[0]), pltpu.make_async_copy(cot_hbm, cot_ref, sems.at[1])]
    for copy in copies:
        copy.start()
    done_ref[...] = jnp.zeros(done_ref.shape, done_ref.dtype)
    for copy in copies:
        copy.wait()


def merge_kernel(*refs):
    packs, (out, features) = refs[:-3], refs[-2:]
    places = len(packs)
    size, both = packs[0].shape
    head_dim = both // 2
    rows, keep = head_dim, size - ID_ROWS
    lane = lax.broadcasted_iota(jnp.int32, (rows, head_dim), 1).astype(jnp.float32)
    for p, pack in enumerate(packs):
        out[p * keep : (p + 1) * keep, :] = pack[:keep, :]
        ids = pack[keep:, :head_dim].astype(jnp.float32)[0:1]
        hit = jnp.transpose(jnp.broadcast_to(ids, (head_dim, rows))) == lane
        other = jnp.where(hit, 0.0, MASK).astype(jnp.bfloat16)
        features[p * rows : (p + 1) * rows, :head_dim] = other
        features[p * rows : (p + 1) * rows, head_dim:] = jnp.where(hit, 1.0, 0.0).astype(jnp.bfloat16)
        at = places * keep + p // 2 * rows
        out[at : at + rows, p % 2 * head_dim : (p % 2 + 1) * head_dim] = other


def attend_kernel(groups, members, places, scale, *refs):
    half = groups // 2
    packs, features, merged, refs = refs[:groups], refs[groups : groups + 2], refs[groups + 2 : groups + 2 * members], refs[groups + 2 * members :]
    queries, outs = refs[: len(places)], refs[-len(places) :]
    rows, part = outs[0].shape
    size, both = packs[0].shape
    head_dim = both // 2
    keep = size - ID_ROWS
    nt = (((1,), (1,)), ((), ()))
    blocks = [(pack, 0) for pack in packs] + [(other, p * keep) for other in merged for p in range(half)]
    other_clip = [(ref, p * rows, 0) for ref in features for p in range(half)]
    other_clip += [(other, half * keep + p // 2 * rows, p % 2 * head_dim) for other in merged for p in range(half)]
    same = jnp.concatenate([features[p // half][p % half * rows : (p % half + 1) * rows, head_dim:] for p in places], axis=0)

    def products(i):
        q = jnp.concatenate([query[i * rows : (i + 1) * rows, :] for query in queries], axis=0)
        q_masked = jnp.concatenate([q[:, head_dim:], same], axis=1)
        scores, slopes = [], []
        for b in range(0, len(blocks), 2):
            pair = [(ref, at + 2 * i * rows) for ref, at in blocks[b : b + 2]]
            masks = [ref[at : at + rows, col : col + head_dim] for ref, at, col in other_clip[b : b + 2]]
            keys = jnp.concatenate([ref[at : at + rows, :] for ref, at in pair], axis=0)
            masked = [jnp.concatenate([ref[at : at + rows, :head_dim], mask], axis=1) for (ref, at), mask in zip(pair, masks)]
            scores.append(lax.dot_general(q_masked, jnp.concatenate(masked, axis=0), nt, preferred_element_type=jnp.float32))
            slopes.append(lax.dot_general(q, keys, nt, preferred_element_type=jnp.float32))
        return scores, slopes

    def finish(i, scores, slopes):
        best = functools.reduce(jnp.maximum, scores)
        best = jnp.max(best, axis=1, keepdims=True)
        weights = [jnp.exp2((score - best) * (scale * math.log2(math.e))) for score in scores]
        tilted = [weight * slope for weight, slope in zip(weights, slopes)]
        total = 1.0 / jnp.sum(functools.reduce(lambda a, b: a + b, weights), axis=1, keepdims=True)
        weights = jnp.concatenate([weight.astype(jnp.bfloat16) for weight in weights], axis=1)
        tilted = jnp.concatenate([tilt.astype(jnp.bfloat16) for tilt in tilted], axis=1)
        vals = jnp.concatenate([ref[at + (2 * i + 1) * rows : at + (2 * i + 2) * rows, :] for ref, at in blocks], axis=0)
        ones = jnp.ones((vals.shape[0], head_dim), jnp.bfloat16)
        mixed = jnp.dot(weights, vals, preferred_element_type=jnp.float32)
        leaned = jnp.dot(tilted, jnp.concatenate([vals[:, :head_dim], ones], axis=1), preferred_element_type=jnp.float32)
        primal, spread = mixed[:, :head_dim], mixed[:, head_dim:]
        slope_part, weighted = leaned[:, :head_dim], leaned[:, head_dim:]
        out = ((slope_part - weighted * (primal * total)) * scale + spread) * total
        for k, ref in enumerate(outs):
            ref[:, i * head_dim : (i + 1) * head_dim] = out[k * rows : (k + 1) * rows].astype(jnp.bfloat16)

    ready = products(0)
    for i in range(part // head_dim):
        following = products(i + 1) if (i + 1) * head_dim < part else None
        finish(i, *ready)
        ready = following


def part_kernel(members, offsets, tile, ta_ref, w_ref, *refs):
    begun, out_ref = refs[:-1], refs[-1]
    group = group_of(offsets, members)
    width = ta_ref.shape[1]
    place = pl.ds(pl.multiple_of(group * width, width), width)
    for j in range(w_ref.shape[1] // tile):
        cols = slice(j * tile, (j + 1) * tile)
        part = jnp.dot(ta_ref[...], w_ref[place, cols], preferred_element_type=jnp.float32)
        out_ref[:, cols] = begun[0][:, cols] + part if begun else part


def project_kernel(members, offsets, tile, ta_ref, w_ref, begun_ref, cot_ref, projected_ref, grad_ref):
    group = group_of(offsets, members)
    width = ta_ref.shape[1]
    place = pl.ds(pl.multiple_of(group * width, width), width)
    for j in range(w_ref.shape[1] // tile):
        cols = slice(j * tile, (j + 1) * tile)
        projected = begun_ref[:, cols] + jnp.dot(ta_ref[...], w_ref[place, cols], preferred_element_type=jnp.float32)
        projected_ref[:, cols] = projected
        grad_ref[:, cols] = jnp.sum(cot_ref[0, :, cols].astype(jnp.float32) * projected, axis=0, keepdims=True)


def branch_kernel(projected_ref, scale_ref, branch_ref):
    branch_ref[0] = (scale_ref[...] * projected_ref[...]).astype(jnp.bfloat16)


def sum_kernel(factor, *refs):
    terms = [ref[...] for ref in refs[:-1]]
    while len(terms) > 1:
        terms = [terms[i] + terms[i + 1] for i in range(0, len(terms), 2)]
    refs[-1][...] = terms[0] * factor


def exchange_sum(x, partners, factor=1.0):
    n_ctx, n_dp = lax.axis_size("ctx"), lax.axis_size("dp")
    places = [(j, z) for j in range(n_ctx) for z in range(n_dp)]
    terms = [lax.ppermute(x, ("ctx", "dp"), [(j * n_dp + z, (j ^ own) * n_dp + (z ^ other)) for j, z in places]) for own, other in partners]
    return pl.pallas_call(
        functools.partial(sum_kernel, factor),
        out_shape=jax.ShapeDtypeStruct(x.shape, x.dtype),
        compiler_params=pltpu.CompilerParams(vmem_limit_bytes=16 * MIB),
        name="sum",
    )(*terms, x)


def local(queries, keys, values, tangent_queries, tangent_keys, tangent_values, clip_ids, block_order, out_weight, layer_scale, cotangent):
    n_ctx, n_dp = lax.axis_size("ctx"), lax.axis_size("dp")
    rows, features = queries.shape[1:]
    head_dim = features // HEADS
    width = out_weight.shape[1]
    groups = math.gcd(n_ctx, HEADS)
    members = n_ctx // groups
    per_group = HEADS // groups
    vmem = pl.BlockSpec(memory_space=pltpu.VMEM)
    hbm = pl.BlockSpec(memory_space=pltpu.HBM)
    bf16 = jnp.bfloat16

    cross = 1 if members > 1 else 0

    def swap(x, offset):
        return lax.ppermute(x, "ctx", [(j, j ^ offset) for j in range(n_ctx)])

    far = sorted((offset for offset in range(groups) if offset.bit_count() > 1), key=lambda offset: -offset.bit_count())
    near = [offset for offset in range(groups) if offset.bit_count() == 1]
    route = [(0, 0)] + [(offset, offset) for offset in far] + list(zip(near, reversed(near)))
    early, late = [*range(1 + len(far))], [*range(1 + len(far), groups)]

    def send(x, place):
        offset = [route[place][odd_one(j // members, j % members)] for j in range(n_ctx)]
        return lax.ppermute(x, "ctx", [(j, j ^ (offset[j] * members + cross)) for j in range(n_ctx)])

    kv_pack = (2 * per_group * rows + ID_ROWS, 2 * head_dim)
    q_pack = (per_group * rows, 2 * head_dim)

    def in_hbm(x):
        return pltpu.with_memory_space_constraint(x, pltpu.HBM)

    def pack(name, places, shape, turns, with_ids, sources):
        return pl.pallas_call(
            functools.partial(pack_kernel, [route[place] for place in places], members, turns, with_ids),
            out_shape=[pltpu.VMEM(shape, bf16)] * len(places),
            in_specs=[hbm] * (2 + len(sources)),
            out_specs=[vmem] * len(places),
            scratch_shapes=[
                pltpu.VMEM((len(sources), len(places), rows, per_group * head_dim), bf16),
                pltpu.SemaphoreType.DMA((len(sources), len(places))),
                pltpu.SMEM(block_order.shape, jnp.int32),
                pltpu.VMEM(clip_ids.shape, jnp.int32),
                pltpu.SemaphoreType.DMA((2,)),
            ],
            compiler_params=pltpu.CompilerParams(vmem_limit_bytes=16 * MIB),
            name=name,
        )(*map(in_hbm, (block_order, clip_ids) + sources))

    key_sources = (keys, tangent_keys, values, tangent_values)
    far_kv = pack("pack_far", early[1:], kv_pack, (True, False), True, key_sources)
    near_kv = pack("pack_near", [0, *late], kv_pack, (True, False), True, key_sources)
    kv = [near_kv[0], *far_kv, *near_kv[1:]]
    q = list(pack("pack_queries", range(groups), q_pack, (True,), False, (tangent_queries, queries)))

    weight, cot, staged = pl.pallas_call(
        stage_kernel,
        out_shape=[pltpu.VMEM(out_weight.shape, bf16), pltpu.VMEM(cotangent.shape, bf16), pltpu.VMEM((8, 128), jnp.float32)],
        in_specs=[hbm, hbm, vmem],
        out_specs=[vmem] * 3,
        scratch_shapes=[pltpu.SemaphoreType.DMA((2,))],
        compiler_params=pltpu.CompilerParams(vmem_limit_bytes=16 * MIB),
        name="stage",
    )(in_hbm(out_weight), in_hbm(cotangent), q[0])

    def exchange(sent):
        return [sent[0]] + [send(sent[place], place) for place in range(1, groups)]

    kv = exchange(kv)
    q = exchange(q)

    def merge(name, packs, after):
        places = len(packs)
        return pl.pallas_call(
            merge_kernel,
            out_shape=[
                jax.ShapeDtypeStruct((places * 2 * per_group * rows + places // 2 * rows, 2 * head_dim), bf16),
                jax.ShapeDtypeStruct((places * rows, 2 * head_dim), bf16),
            ],
            in_specs=[vmem] * (places + 1),
            out_specs=[vmem] * 2,
            compiler_params=pltpu.CompilerParams(vmem_limit_bytes=16 * MIB),
            name=name,
        )(*packs, after)

    merged_first, features_first = merge("merge_first", kv[: groups // 2], q[0])
    merged_last, features_last = merge("merge_last", kv[groups // 2 :], staged)
    others = [swap(merged, s) for s in range(1, members) for merged in (merged_first, merged_last)]
    arrived = pl.pallas_call(
        arrived_kernel,
        out_shape=jax.ShapeDtypeStruct((8, 128), jnp.float32),
        in_specs=[vmem] * len(early),
        out_specs=vmem,
        compiler_params=pltpu.CompilerParams(vmem_limit_bytes=16 * MIB),
        cost_estimate=pl.CostEstimate(flops=10**11, bytes_accessed=MIB, transcendentals=0),
        name="arrived",
    )(*(q[place] for place in early))

    def attend(name, places, *after):
        return pl.pallas_call(
            functools.partial(attend_kernel, groups, members, places, head_dim ** (-0.5)),
            out_shape=[jax.ShapeDtypeStruct((rows, per_group * head_dim), bf16)] * len(places),
            in_specs=[vmem] * (groups + 2 * members + len(places) + len(after)),
            out_specs=[vmem] * len(places),
            compiler_params=pltpu.CompilerParams(vmem_limit_bytes=24 * MIB),
            name=name,
        )(*kv, features_first, features_last, *others, *(q[place] for place in places), *after)

    done = dict(zip(early, attend("attend_early", early, arrived)))
    for place in early[1:]:
        done[place] = send(done[place], place)
    done.update(zip(late, attend("attend_late", late)))
    for place in late:
        done[place] = send(done[place], place)
    arrivals = [*early, *late]
    begun = None
    for place in arrivals[:-1]:
        begun = pl.pallas_call(
            functools.partial(part_kernel, members, route[place], 512),
            out_shape=jax.ShapeDtypeStruct((rows, width), jnp.float32),
            in_specs=[vmem] * (2 + (begun is not None)),
            out_specs=vmem,
            compiler_params=pltpu.CompilerParams(vmem_limit_bytes=16 * MIB),
            name=f"part{place}",
        )(done[place], weight, *([] if begun is None else [begun]))
    projected, grad = pl.pallas_call(
        functools.partial(project_kernel, members, route[arrivals[-1]], 512),
        out_shape=[jax.ShapeDtypeStruct((rows, width), jnp.float32), jax.ShapeDtypeStruct((1, width), jnp.float32)],
        in_specs=[vmem] * 4,
        out_specs=[vmem] * 2,
        compiler_params=pltpu.CompilerParams(vmem_limit_bytes=16 * MIB),
        name="project",
    )(done[arrivals[-1]], weight, begun, cot)
    branch = pl.pallas_call(
        branch_kernel,
        out_shape=jax.ShapeDtypeStruct((1, rows, width), bf16),
        in_specs=[vmem] * 2,
        out_specs=vmem,
        compiler_params=pltpu.CompilerParams(vmem_limit_bytes=16 * MIB),
        name="branch",
    )(projected, layer_scale[None, :])
    summed = exchange_sum(grad, [(s, 0) for s in reversed(range(1, members))])
    summed = exchange_sum(summed, [(offset + cross, 0) for offset in reversed(range(members, n_ctx, members))])
    factor = 1.0 / math.sqrt(n_ctx * n_dp * rows)
    offsets = [1 << k for k in range(n_dp.bit_length() - 1)]
    for offset in offsets:
        summed = exchange_sum(summed, [(cross, offset)], factor if offset == offsets[-1] else 1.0)
    return branch, summed[0]


def solution(mesh):
    tokens = P("dp", "ctx", None)
    in_specs = (tokens,) * 6 + (P("dp", "ctx"), P(), P(), P(), tokens)
    return jax.shard_map(local, mesh=mesh, in_specs=in_specs, out_specs=(tokens, P()), check_vma=False)
```

```python
import functools
import math

import jax
import jax.numpy as jnp
from jax import lax
from jax.experimental import pallas as pl
from jax.experimental.pallas import tpu as pltpu
from jax.sharding import PartitionSpec as P

HEADS = 12
ID_ROWS = 16
MASK = -3e38
MIB = 2**20


def frequencies(lane, half):
    index = lane % half
    low = 1 << (half.bit_length() // 2)

    def pick(part, count, step):
        factor = jnp.ones(lane.shape, jnp.float32)
        for k in range(1, count):
            factor = jnp.where(part == k, 10000.0 ** (-k * step / half), factor)
        return factor

    return pick(index // low, half // low, low) * pick(index % low, low, 1)


def tables(blocks, rows, head_dim):
    lane = lax.broadcasted_iota(jnp.int32, (8, head_dim), 1)
    line = lax.broadcasted_iota(jnp.int32, (8, head_dim), 0)
    frequency = frequencies(lane, head_dim // 2)
    steps = rows // 8
    positions = [line] + [8 * (line + 8 * k) for k in range(steps // 8)] + [rows * (line + 8 * k) for k in range(blocks // 8)]
    angles = jnp.concatenate([position.astype(jnp.float32) * frequency for position in positions], axis=0)
    return jnp.cos(angles), jnp.sin(angles)


def rotation(block, rows, head_dim, cosines, sines):
    half = head_dim // 2
    steps = rows // 8
    lane = lax.broadcasted_iota(jnp.int32, (8, head_dim), 1)
    firsts = cosines.shape[0] - 8 - steps
    here = lax.broadcasted_iota(jnp.int32, (firsts, head_dim), 0) == block
    cos_first = jnp.sum(jnp.where(here, cosines[8 + steps :], 0.0), axis=0, keepdims=True)
    sin_first = jnp.sum(jnp.where(here, sines[8 + steps :], 0.0), axis=0, keepdims=True)
    cos_v, sin_v = cosines[:8], sines[:8]
    cos_8u = cos_first * cosines[8 : 8 + steps] - sin_first * sines[8 : 8 + steps]
    sin_8u = sin_first * cosines[8 : 8 + steps] + cos_first * sines[8 : 8 + steps]
    cos_rows, sin_rows = [], []
    for u in range(steps):
        cos_u, sin_u = cos_8u[u : u + 1], sin_8u[u : u + 1]
        cos_rows.append(cos_u * cos_v - sin_u * sin_v)
        sin_rows.append(jnp.where(lane < half, -1.0, 1.0) * (sin_u * cos_v + cos_u * sin_v))
    return jnp.concatenate(cos_rows, axis=0), jnp.concatenate(sin_rows, axis=0)


def odd_one(group, place):
    bits = group
    for shift in (4, 2, 1):
        bits = bits ^ (bits >> shift)
    return ((bits & 1) + place) % 2


def group_of(offsets, members):
    me = lax.axis_index("ctx")
    group = me // members
    even, odd = offsets
    return group ^ (even if even == odd else jnp.where(odd_one(group, me % members) == 0, even, odd))


def pack_kernel(offsets, members, turns, with_ids, order_hbm, ids_hbm, *refs):
    n_in = 2 * len(turns)
    sources, outs, (scratch, in_sems, order_ref, ids_ref, small_sems) = refs[:n_in], refs[n_in:-5], refs[-5:]
    rows, part = scratch.shape[2:]
    head_dim = outs[0].shape[1] // 2
    per_group = part // head_dim
    small = [pltpu.make_async_copy(order_hbm, order_ref, small_sems.at[0]), pltpu.make_async_copy(ids_hbm, ids_ref, small_sems.at[1])]
    for load in small:
        load.start()
    loads = {}
    for t, source in enumerate(sources):
        for p, pair in enumerate(offsets):
            column = pl.multiple_of(group_of(pair, members) * part, part)
            loads[t, p] = pltpu.make_async_copy(source.at[0, :, pl.ds(column, part)], scratch.at[t, p], in_sems.at[t, p])
            loads[t, p].start()
    cosines, sines = tables(order_ref.shape[0], rows, head_dim)
    small[0].wait()
    cosine, sine = rotation(order_ref[lax.axis_index("ctx")], rows, head_dim, cosines, sines)

    def turned(x):
        x = x.astype(jnp.float32)
        return (x * cosine + pltpu.roll(x, head_dim // 2, 1) * sine).astype(jnp.bfloat16)

    small[1].wait()
    if with_ids:
        ids = jnp.broadcast_to(ids_ref[...].astype(jnp.float32), (ID_ROWS, rows)).astype(jnp.bfloat16)
        for out in outs:
            out[per_group * len(turns) * rows :, :head_dim] = ids
            out[per_group * len(turns) * rows :, head_dim:] = ids
    for t in range(n_in):
        for p, out in enumerate(outs):
            loads[t, p].wait()
            for i in range(per_group):
                x = scratch[t, p, :, i * head_dim : (i + 1) * head_dim]
                at = (i * len(turns) + t // 2) * rows
                out[at : at + rows, t % 2 * head_dim : (t % 2 + 1) * head_dim] = turned(x) if turns[t // 2] else x


def arrived_kernel(*refs):
    refs[-1][...] = jnp.zeros(refs[-1].shape, refs[-1].dtype)


def stage_kernel(w_hbm, cot_hbm, after_ref, w_ref, cot_ref, done_ref, sems):
    copies = [pltpu.make_async_copy(w_hbm, w_ref, sems.at[0]), pltpu.make_async_copy(cot_hbm, cot_ref, sems.at[1])]
    for copy in copies:
        copy.start()
    done_ref[...] = jnp.zeros(done_ref.shape, done_ref.dtype)
    for copy in copies:
        copy.wait()


def merge_kernel(*refs):
    packs, (out, features) = refs[:-3], refs[-2:]
    places = len(packs)
    size, both = packs[0].shape
    head_dim = both // 2
    rows, keep = head_dim, size - ID_ROWS
    lane = lax.broadcasted_iota(jnp.int32, (rows, head_dim), 1).astype(jnp.float32)
    for p, pack in enumerate(packs):
        out[p * keep : (p + 1) * keep, :] = pack[:keep, :]
        ids = pack[keep:, :head_dim].astype(jnp.float32)[0:1]
        hit = jnp.transpose(jnp.broadcast_to(ids, (head_dim, rows))) == lane
        other = jnp.where(hit, 0.0, MASK).astype(jnp.bfloat16)
        features[p * rows : (p + 1) * rows, :head_dim] = other
        features[p * rows : (p + 1) * rows, head_dim:] = jnp.where(hit, 1.0, 0.0).astype(jnp.bfloat16)
        at = places * keep + p // 2 * rows
        out[at : at + rows, p % 2 * head_dim : (p % 2 + 1) * head_dim] = other


def attend_kernel(groups, members, places, scale, *refs):
    half = groups // 2
    packs, features, merged, refs = refs[:groups], refs[groups : groups + 2], refs[groups + 2 : groups + 2 * members], refs[groups + 2 * members :]
    queries, outs = refs[: len(places)], refs[-len(places) :]
    rows, part = outs[0].shape
    size, both = packs[0].shape
    head_dim = both // 2
    keep = size - ID_ROWS
    nt = (((1,), (1,)), ((), ()))
    blocks = [(pack, 0) for pack in packs] + [(other, p * keep) for other in merged for p in range(half)]
    other_clip = [(ref, p * rows, 0) for ref in features for p in range(half)]
    other_clip += [(other, half * keep + p // 2 * rows, p % 2 * head_dim) for other in merged for p in range(half)]
    same = jnp.concatenate([features[p // half][p % half * rows : (p % half + 1) * rows, head_dim:] for p in places], axis=0)

    def products(i):
        q = jnp.concatenate([query[i * rows : (i + 1) * rows, :] for query in queries], axis=0)
        q_masked = jnp.concatenate([q[:, head_dim:], same], axis=1)
        scores, slopes = [], []
        for b in range(0, len(blocks), 2):
            pair = [(ref, at + 2 * i * rows) for ref, at in blocks[b : b + 2]]
            masks = [ref[at : at + rows, col : col + head_dim] for ref, at, col in other_clip[b : b + 2]]
            keys = jnp.concatenate([ref[at : at + rows, :] for ref, at in pair], axis=0)
            masked = [jnp.concatenate([ref[at : at + rows, :head_dim], mask], axis=1) for (ref, at), mask in zip(pair, masks)]
            scores.append(lax.dot_general(q_masked, jnp.concatenate(masked, axis=0), nt, preferred_element_type=jnp.float32))
            slopes.append(lax.dot_general(q, keys, nt, preferred_element_type=jnp.float32))
        return scores, slopes

    def finish(i, scores, slopes):
        best = functools.reduce(jnp.maximum, scores)
        best = jnp.max(best, axis=1, keepdims=True)
        weights = [jnp.exp2((score - best) * (scale * math.log2(math.e))) for score in scores]
        tilted = [weight * slope for weight, slope in zip(weights, slopes)]
        total = 1.0 / jnp.sum(functools.reduce(lambda a, b: a + b, weights), axis=1, keepdims=True)
        weights = jnp.concatenate([weight.astype(jnp.bfloat16) for weight in weights], axis=1)
        tilted = jnp.concatenate([tilt.astype(jnp.bfloat16) for tilt in tilted], axis=1)
        vals = jnp.concatenate([ref[at + (2 * i + 1) * rows : at + (2 * i + 2) * rows, :] for ref, at in blocks], axis=0)
        ones = jnp.ones((vals.shape[0], head_dim), jnp.bfloat16)
        mixed = jnp.dot(weights, vals, preferred_element_type=jnp.float32)
        leaned = jnp.dot(tilted, jnp.concatenate([vals[:, :head_dim], ones], axis=1), preferred_element_type=jnp.float32)
        primal, spread = mixed[:, :head_dim], mixed[:, head_dim:]
        slope_part, weighted = leaned[:, :head_dim], leaned[:, head_dim:]
        out = ((slope_part - weighted * (primal * total)) * scale + spread) * total
        for k, ref in enumerate(outs):
            ref[:, i * head_dim : (i + 1) * head_dim] = out[k * rows : (k + 1) * rows].astype(jnp.bfloat16)

    ready = products(0)
    for i in range(part // head_dim):
        following = products(i + 1) if (i + 1) * head_dim < part else None
        finish(i, *ready)
        ready = following


def part_kernel(members, offsets, tile, ta_ref, w_ref, *refs):
    begun, out_ref = refs[:-1], refs[-1]
    group = group_of(offsets, members)
    width = ta_ref.shape[1]
    place = pl.ds(pl.multiple_of(group * width, width), width)
    for j in range(w_ref.shape[1] // tile):
        cols = slice(j * tile, (j + 1) * tile)
        part = jnp.dot(ta_ref[...], w_ref[place, cols], preferred_element_type=jnp.float32)
        out_ref[:, cols] = begun[0][:, cols] + part if begun else part


def project_kernel(members, offsets, tile, ta_ref, w_ref, begun_ref, cot_ref, projected_ref, grad_ref):
    group = group_of(offsets, members)
    width = ta_ref.shape[1]
    place = pl.ds(pl.multiple_of(group * width, width), width)
    for j in range(w_ref.shape[1] // tile):
        cols = slice(j * tile, (j + 1) * tile)
        projected = begun_ref[:, cols] + jnp.dot(ta_ref[...], w_ref[place, cols], preferred_element_type=jnp.float32)
        projected_ref[:, cols] = projected
        grad_ref[:, cols] = jnp.sum(cot_ref[0, :, cols].astype(jnp.float32) * projected, axis=0, keepdims=True)


def branch_kernel(projected_ref, scale_ref, branch_ref):
    branch_ref[0] = (scale_ref[...] * projected_ref[...]).astype(jnp.bfloat16)


def sum_kernel(factor, *refs):
    terms = [ref[...] for ref in refs[:-1]]
    while len(terms) > 1:
        terms = [terms[i] + terms[i + 1] for i in range(0, len(terms), 2)]
    refs[-1][...] = terms[0] * factor


def exchange_sum(x, partners, factor=1.0):
    n_ctx, n_dp = lax.axis_size("ctx"), lax.axis_size("dp")
    places = [(j, z) for j in range(n_ctx) for z in range(n_dp)]
    terms = [lax.ppermute(x, ("ctx", "dp"), [(j * n_dp + z, (j ^ own) * n_dp + (z ^ other)) for j, z in places]) for own, other in partners]
    return pl.pallas_call(
        functools.partial(sum_kernel, factor),
        out_shape=jax.ShapeDtypeStruct(x.shape, x.dtype),
        compiler_params=pltpu.CompilerParams(vmem_limit_bytes=16 * MIB),
        name="sum",
    )(*terms, x)


def local(queries, keys, values, tangent_queries, tangent_keys, tangent_values, clip_ids, block_order, out_weight, layer_scale, cotangent):
    n_ctx, n_dp = lax.axis_size("ctx"), lax.axis_size("dp")
    rows, features = queries.shape[1:]
    head_dim = features // HEADS
    width = out_weight.shape[1]
    groups = math.gcd(n_ctx, HEADS)
    members = n_ctx // groups
    per_group = HEADS // groups
    vmem = pl.BlockSpec(memory_space=pltpu.VMEM)
    hbm = pl.BlockSpec(memory_space=pltpu.HBM)
    bf16 = jnp.bfloat16

    cross = 1 if members > 1 else 0

    def swap(x, offset):
        return lax.ppermute(x, "ctx", [(j, j ^ offset) for j in range(n_ctx)])

    far = sorted((offset for offset in range(groups) if offset.bit_count() > 1), key=lambda offset: -offset.bit_count())
    near = [offset for offset in range(groups) if offset.bit_count() == 1]
    route = [(0, 0)] + [(offset, offset) for offset in far] + list(zip(near, reversed(near)))
    early, late = [*range(1 + len(far))], [*range(1 + len(far), groups)]

    def send(x, place):
        offset = [route[place][odd_one(j // members, j % members)] for j in range(n_ctx)]
        return lax.ppermute(x, "ctx", [(j, j ^ (offset[j] * members + cross)) for j in range(n_ctx)])

    kv_pack = (2 * per_group * rows + ID_ROWS, 2 * head_dim)
    q_pack = (per_group * rows, 2 * head_dim)

    def in_hbm(x):
        return pltpu.with_memory_space_constraint(x, pltpu.HBM)

    def pack(name, places, shape, turns, with_ids, sources):
        return pl.pallas_call(
            functools.partial(pack_kernel, [route[place] for place in places], members, turns, with_ids),
            out_shape=[pltpu.VMEM(shape, bf16)] * len(places),
            in_specs=[hbm] * (2 + len(sources)),
            out_specs=[vmem] * len(places),
            scratch_shapes=[
                pltpu.VMEM((len(sources), len(places), rows, per_group * head_dim), bf16),
                pltpu.SemaphoreType.DMA((len(sources), len(places))),
                pltpu.SMEM(block_order.shape, jnp.int32),
                pltpu.VMEM(clip_ids.shape, jnp.int32),
                pltpu.SemaphoreType.DMA((2,)),
            ],
            compiler_params=pltpu.CompilerParams(vmem_limit_bytes=16 * MIB),
            name=name,
        )(*map(in_hbm, (block_order, clip_ids) + sources))

    key_sources = (keys, tangent_keys, values, tangent_values)
    far_kv = pack("pack_far", early[1:], kv_pack, (True, False), True, key_sources)
    near_kv = pack("pack_near", [0, *late], kv_pack, (True, False), True, key_sources)
    kv = [near_kv[0], *far_kv, *near_kv[1:]]
    q = list(pack("pack_queries", range(groups), q_pack, (True,), False, (tangent_queries, queries)))

    weight, cot, staged = pl.pallas_call(
        stage_kernel,
        out_shape=[pltpu.VMEM(out_weight.shape, bf16), pltpu.VMEM(cotangent.shape, bf16), pltpu.VMEM((8, 128), jnp.float32)],
        in_specs=[hbm, hbm, vmem],
        out_specs=[vmem] * 3,
        scratch_shapes=[pltpu.SemaphoreType.DMA((2,))],
        compiler_params=pltpu.CompilerParams(vmem_limit_bytes=16 * MIB),
        name="stage",
    )(in_hbm(out_weight), in_hbm(cotangent), q[0])

    def exchange(sent):
        return [sent[0]] + [send(sent[place], place) for place in range(1, groups)]

    kv = exchange(kv)
    q = exchange(q)

    def merge(name, packs, after):
        places = len(packs)
        return pl.pallas_call(
            merge_kernel,
            out_shape=[
                jax.ShapeDtypeStruct((places * 2 * per_group * rows + places // 2 * rows, 2 * head_dim), bf16),
                jax.ShapeDtypeStruct((places * rows, 2 * head_dim), bf16),
            ],
            in_specs=[vmem] * (places + 1),
            out_specs=[vmem] * 2,
            compiler_params=pltpu.CompilerParams(vmem_limit_bytes=16 * MIB),
            name=name,
        )(*packs, after)

    merged_first, features_first = merge("merge_first", kv[: groups // 2], q[0])
    merged_last, features_last = merge("merge_last", kv[groups // 2 :], staged)
    others = [swap(merged, s) for s in range(1, members) for merged in (merged_first, merged_last)]
    arrived = pl.pallas_call(
        arrived_kernel,
        out_shape=jax.ShapeDtypeStruct((8, 128), jnp.float32),
        in_specs=[vmem] * len(early),
        out_specs=vmem,
        compiler_params=pltpu.CompilerParams(vmem_limit_bytes=16 * MIB),
        cost_estimate=pl.CostEstimate(flops=10**11, bytes_accessed=MIB, transcendentals=0),
        name="arrived",
    )(*(q[place] for place in early))

    def attend(name, places, *after):
        return pl.pallas_call(
            functools.partial(attend_kernel, groups, members, places, head_dim ** (-0.5)),
            out_shape=[jax.ShapeDtypeStruct((rows, per_group * head_dim), bf16)] * len(places),
            in_specs=[vmem] * (groups + 2 * members + len(places) + len(after)),
            out_specs=[vmem] * len(places),
            compiler_params=pltpu.CompilerParams(vmem_limit_bytes=24 * MIB),
            name=name,
        )(*kv, features_first, features_last, *others, *(q[place] for place in places), *after)

    done = dict(zip(early, attend("attend_early", early, arrived)))
    for place in early[1:]:
        done[place] = send(done[place], place)
    done.update(zip(late, attend("attend_late", late)))
    for place in late:
        done[place] = send(done[place], place)
    arrivals = [*early, *late]
    begun = None
    for place in arrivals[:-1]:
        begun = pl.pallas_call(
            functools.partial(part_kernel, members, route[place], 512),
            out_shape=jax.ShapeDtypeStruct((rows, width), jnp.float32),
            in_specs=[vmem] * (2 + (begun is not None)),
            out_specs=vmem,
            compiler_params=pltpu.CompilerParams(vmem_limit_bytes=16 * MIB),
            name=f"part{place}",
        )(done[place], weight, *([] if begun is None else [begun]))
    projected, grad = pl.pallas_call(
        functools.partial(project_kernel, members, route[arrivals[-1]], 512),
        out_shape=[jax.ShapeDtypeStruct((rows, width), jnp.float32), jax.ShapeDtypeStruct((1, width), jnp.float32)],
        in_specs=[vmem] * 4,
        out_specs=[vmem] * 2,
        compiler_params=pltpu.CompilerParams(vmem_limit_bytes=16 * MIB),
        name="project",
    )(done[arrivals[-1]], weight, begun, cot)
    branch = pl.pallas_call(
        branch_kernel,
        out_shape=jax.ShapeDtypeStruct((1, rows, width), bf16),
        in_specs=[vmem] * 2,
        out_specs=vmem,
        compiler_params=pltpu.CompilerParams(vmem_limit_bytes=16 * MIB),
        name="branch",
    )(projected, layer_scale[None, :])
    summed = exchange_sum(grad, [(s, 0) for s in reversed(range(1, members))])
    summed = exchange_sum(summed, [(offset + cross, 0) for offset in reversed(range(members, n_ctx, members))])
    factor = 1.0 / math.sqrt(n_ctx * n_dp * rows)
    offsets = [1 << k for k in range(n_dp.bit_length() - 1)]
    for offset in offsets:
        summed = exchange_sum(summed, [(cross, offset)], factor if offset == offsets[-1] else 1.0)
    return branch, summed[0]


def solution(mesh):
    tokens = P("dp", "ctx", None)
    in_specs = (tokens,) * 6 + (P("dp", "ctx"), P(), P(), P(), tokens)
    return jax.shard_map(local, mesh=mesh, in_specs=in_specs, out_specs=(tokens, P()), check_vma=False)
```

```python
import functools
import math

import jax
import jax.numpy as jnp
from jax import lax
from jax.experimental import pallas as pl
from jax.experimental.pallas import tpu as pltpu
from jax.sharding import PartitionSpec as P

HEADS = 12
ID_ROWS = 16
MASK = -3e38
MIB = 2**20


def frequencies(lane, half):
    index = lane % half
    low = 1 << (half.bit_length() // 2)

    def pick(part, count, step):
        factor = jnp.ones(lane.shape, jnp.float32)
        for k in range(1, count):
            factor = jnp.where(part == k, 10000.0 ** (-k * step / half), factor)
        return factor

    return pick(index // low, half // low, low) * pick(index % low, low, 1)


def tables(blocks, rows, head_dim):
    lane = lax.broadcasted_iota(jnp.int32, (8, head_dim), 1)
    line = lax.broadcasted_iota(jnp.int32, (8, head_dim), 0)
    frequency = frequencies(lane, head_dim // 2)
    steps = rows // 8
    positions = [line] + [8 * (line + 8 * k) for k in range(steps // 8)] + [rows * (line + 8 * k) for k in range(blocks // 8)]
    angles = jnp.concatenate([position.astype(jnp.float32) * frequency for position in positions], axis=0)
    return jnp.cos(angles), jnp.sin(angles)


def rotation(block, rows, head_dim, cosines, sines):
    half = head_dim // 2
    steps = rows // 8
    lane = lax.broadcasted_iota(jnp.int32, (8, head_dim), 1)
    firsts = cosines.shape[0] - 8 - steps
    here = lax.broadcasted_iota(jnp.int32, (firsts, head_dim), 0) == block
    cos_first = jnp.sum(jnp.where(here, cosines[8 + steps :], 0.0), axis=0, keepdims=True)
    sin_first = jnp.sum(jnp.where(here, sines[8 + steps :], 0.0), axis=0, keepdims=True)
    cos_v, sin_v = cosines[:8], sines[:8]
    cos_8u = cos_first * cosines[8 : 8 + steps] - sin_first * sines[8 : 8 + steps]
    sin_8u = sin_first * cosines[8 : 8 + steps] + cos_first * sines[8 : 8 + steps]
    cos_rows, sin_rows = [], []
    for u in range(steps):
        cos_u, sin_u = cos_8u[u : u + 1], sin_8u[u : u + 1]
        cos_rows.append(cos_u * cos_v - sin_u * sin_v)
        sin_rows.append(jnp.where(lane < half, -1.0, 1.0) * (sin_u * cos_v + cos_u * sin_v))
    return jnp.concatenate(cos_rows, axis=0), jnp.concatenate(sin_rows, axis=0)


def odd_one(group, place):
    bits = group
    for shift in (4, 2, 1):
        bits = bits ^ (bits >> shift)
    return ((bits & 1) + place) % 2


def group_of(offsets, members):
    me = lax.axis_index("ctx")
    group = me // members
    even, odd = offsets
    return group ^ (even if even == odd else jnp.where(odd_one(group, me % members) == 0, even, odd))


def pack_kernel(offsets, members, turns, with_ids, order_hbm, ids_hbm, *refs):
    n_in = 2 * len(turns)
    sources, outs, (scratch, in_sems, order_ref, ids_ref, small_sems) = refs[:n_in], refs[n_in:-5], refs[-5:]
    rows, part = scratch.shape[2:]
    head_dim = outs[0].shape[1] // 2
    per_group = part // head_dim
    small = [pltpu.make_async_copy(order_hbm, order_ref, small_sems.at[0]), pltpu.make_async_copy(ids_hbm, ids_ref, small_sems.at[1])]
    for load in small:
        load.start()
    loads = {}
    for t, source in enumerate(sources):
        for p, pair in enumerate(offsets):
            column = pl.multiple_of(group_of(pair, members) * part, part)
            loads[t, p] = pltpu.make_async_copy(source.at[0, :, pl.ds(column, part)], scratch.at[t, p], in_sems.at[t, p])
            loads[t, p].start()
    cosines, sines = tables(order_ref.shape[0], rows, head_dim)
    def store(t, change):
        for p, out in enumerate(outs):
            loads[t, p].wait()
            for i in range(per_group):
                at = (i * len(turns) + t // 2) * rows
                out[at : at + rows, t % 2 * head_dim : (t % 2 + 1) * head_dim] = change(scratch[t, p, :, i * head_dim : (i + 1) * head_dim])

    for t in range(n_in):
        if not turns[t // 2]:
            store(t, lambda x: x)
    small[0].wait()
    cosine, sine = rotation(order_ref[lax.axis_index("ctx")], rows, head_dim, cosines, sines)

    def turned(x):
        x = x.astype(jnp.float32)
        return (x * cosine + pltpu.roll(x, head_dim // 2, 1) * sine).astype(jnp.bfloat16)

    for t in range(n_in):
        if turns[t // 2]:
            store(t, turned)
    small[1].wait()
    if with_ids:
        ids = jnp.broadcast_to(ids_ref[...].astype(jnp.float32), (ID_ROWS, rows)).astype(jnp.bfloat16)
        for out in outs:
            out[per_group * len(turns) * rows :, :head_dim] = ids
            out[per_group * len(turns) * rows :, head_dim:] = ids


def arrived_kernel(*refs):
    refs[-1][...] = jnp.zeros(refs[-1].shape, refs[-1].dtype)


def stage_kernel(w_hbm, cot_hbm, after_ref, w_ref, cot_ref, done_ref, sems):
    copies = [pltpu.make_async_copy(w_hbm, w_ref, sems.at[0]), pltpu.make_async_copy(cot_hbm, cot_ref, sems.at[1])]
    for copy in copies:
        copy.start()
    done_ref[...] = jnp.zeros(done_ref.shape, done_ref.dtype)
    for copy in copies:
        copy.wait()


def merge_kernel(*refs):
    packs, (out, features) = refs[:-3], refs[-2:]
    places = len(packs)
    size, both = packs[0].shape
    head_dim = both // 2
    rows, keep = head_dim, size - ID_ROWS
    lane = lax.broadcasted_iota(jnp.int32, (rows, head_dim), 1).astype(jnp.float32)
    for p, pack in enumerate(packs):
        out[p * keep : (p + 1) * keep, :] = pack[:keep, :]
        ids = pack[keep:, :head_dim].astype(jnp.float32)[0:1]
        hit = jnp.transpose(jnp.broadcast_to(ids, (head_dim, rows))) == lane
        other = jnp.where(hit, 0.0, MASK).astype(jnp.bfloat16)
        features[p * rows : (p + 1) * rows, :head_dim] = other
        features[p * rows : (p + 1) * rows, head_dim:] = jnp.where(hit, 1.0, 0.0).astype(jnp.bfloat16)
        at = places * keep + p // 2 * rows
        out[at : at + rows, p % 2 * head_dim : (p % 2 + 1) * head_dim] = other


def attend_kernel(groups, members, places, scale, *refs):
    half = groups // 2
    packs, features, merged, refs = refs[:groups], refs[groups : groups + 2], refs[groups + 2 : groups + 2 * members], refs[groups + 2 * members :]
    queries, outs = refs[: len(places)], refs[-len(places) :]
    rows, part = outs[0].shape
    size, both = packs[0].shape
    head_dim = both // 2
    keep = size - ID_ROWS
    nt = (((1,), (1,)), ((), ()))
    blocks = [(pack, 0) for pack in packs] + [(other, p * keep) for other in merged for p in range(half)]
    other_clip = [(ref, p * rows, 0) for ref in features for p in range(half)]
    other_clip += [(other, half * keep + p // 2 * rows, p % 2 * head_dim) for other in merged for p in range(half)]
    same = jnp.concatenate([features[p // half][p % half * rows : (p % half + 1) * rows, head_dim:] for p in places], axis=0)

    def products(i):
        q = jnp.concatenate([query[i * rows : (i + 1) * rows, :] for query in queries], axis=0)
        q_masked = jnp.concatenate([q[:, head_dim:], same], axis=1)
        scores, slopes = [], []
        for b in range(0, len(blocks), 2):
            pair = [(ref, at + 2 * i * rows) for ref, at in blocks[b : b + 2]]
            masks = [ref[at : at + rows, col : col + head_dim] for ref, at, col in other_clip[b : b + 2]]
            keys = jnp.concatenate([ref[at : at + rows, :] for ref, at in pair], axis=0)
            masked = [jnp.concatenate([ref[at : at + rows, :head_dim], mask], axis=1) for (ref, at), mask in zip(pair, masks)]
            scores.append(lax.dot_general(q_masked, jnp.concatenate(masked, axis=0), nt, preferred_element_type=jnp.float32))
            slopes.append(lax.dot_general(q, keys, nt, preferred_element_type=jnp.float32))
        return scores, slopes

    def finish(i, scores, slopes):
        best = functools.reduce(jnp.maximum, scores)
        best = jnp.max(best, axis=1, keepdims=True)
        weights = [jnp.exp2((score - best) * (scale * math.log2(math.e))) for score in scores]
        tilted = [weight * slope for weight, slope in zip(weights, slopes)]
        total = 1.0 / jnp.sum(functools.reduce(lambda a, b: a + b, weights), axis=1, keepdims=True)
        weights = jnp.concatenate([weight.astype(jnp.bfloat16) for weight in weights], axis=1)
        tilted = jnp.concatenate([tilt.astype(jnp.bfloat16) for tilt in tilted], axis=1)
        vals = jnp.concatenate([ref[at + (2 * i + 1) * rows : at + (2 * i + 2) * rows, :] for ref, at in blocks], axis=0)
        ones = jnp.ones((vals.shape[0], head_dim), jnp.bfloat16)
        mixed = jnp.dot(weights, vals, preferred_element_type=jnp.float32)
        leaned = jnp.dot(tilted, jnp.concatenate([vals[:, :head_dim], ones], axis=1), preferred_element_type=jnp.float32)
        primal, spread = mixed[:, :head_dim], mixed[:, head_dim:]
        slope_part, weighted = leaned[:, :head_dim], leaned[:, head_dim:]
        out = ((slope_part - weighted * (primal * total)) * scale + spread) * total
        for k, ref in enumerate(outs):
            ref[:, i * head_dim : (i + 1) * head_dim] = out[k * rows : (k + 1) * rows].astype(jnp.bfloat16)

    ready = products(0)
    for i in range(part // head_dim):
        following = products(i + 1) if (i + 1) * head_dim < part else None
        finish(i, *ready)
        ready = following


def part_kernel(members, offsets, tile, ta_ref, w_ref, *refs):
    begun, out_ref = refs[:-1], refs[-1]
    group = group_of(offsets, members)
    width = ta_ref.shape[1]
    place = pl.ds(pl.multiple_of(group * width, width), width)
    for j in range(w_ref.shape[1] // tile):
        cols = slice(j * tile, (j + 1) * tile)
        part = jnp.dot(ta_ref[...], w_ref[place, cols], preferred_element_type=jnp.float32)
        out_ref[:, cols] = begun[0][:, cols] + part if begun else part


def project_kernel(members, offsets, tile, ta_ref, w_ref, begun_ref, cot_ref, projected_ref, grad_ref):
    group = group_of(offsets, members)
    width = ta_ref.shape[1]
    place = pl.ds(pl.multiple_of(group * width, width), width)
    for j in range(w_ref.shape[1] // tile):
        cols = slice(j * tile, (j + 1) * tile)
        projected = begun_ref[:, cols] + jnp.dot(ta_ref[...], w_ref[place, cols], preferred_element_type=jnp.float32)
        projected_ref[:, cols] = projected
        grad_ref[:, cols] = jnp.sum(cot_ref[0, :, cols].astype(jnp.float32) * projected, axis=0, keepdims=True)


def branch_kernel(projected_ref, scale_ref, branch_ref):
    branch_ref[0] = (scale_ref[...] * projected_ref[...]).astype(jnp.bfloat16)


def sum_kernel(factor, *refs):
    terms = [ref[...] for ref in refs[:-1]]
    while len(terms) > 1:
        terms = [terms[i] + terms[i + 1] for i in range(0, len(terms), 2)]
    refs[-1][...] = terms[0] * factor


def exchange_sum(x, partners, factor=1.0):
    n_ctx, n_dp = lax.axis_size("ctx"), lax.axis_size("dp")
    places = [(j, z) for j in range(n_ctx) for z in range(n_dp)]
    terms = [lax.ppermute(x, ("ctx", "dp"), [(j * n_dp + z, (j ^ own) * n_dp + (z ^ other)) for j, z in places]) for own, other in partners]
    return pl.pallas_call(
        functools.partial(sum_kernel, factor),
        out_shape=jax.ShapeDtypeStruct(x.shape, x.dtype),
        compiler_params=pltpu.CompilerParams(vmem_limit_bytes=16 * MIB),
        name="sum",
    )(*terms, x)


def local(queries, keys, values, tangent_queries, tangent_keys, tangent_values, clip_ids, block_order, out_weight, layer_scale, cotangent):
    n_ctx, n_dp = lax.axis_size("ctx"), lax.axis_size("dp")
    rows, features = queries.shape[1:]
    head_dim = features // HEADS
    width = out_weight.shape[1]
    groups = math.gcd(n_ctx, HEADS)
    members = n_ctx // groups
    per_group = HEADS // groups
    vmem = pl.BlockSpec(memory_space=pltpu.VMEM)
    hbm = pl.BlockSpec(memory_space=pltpu.HBM)
    bf16 = jnp.bfloat16

    cross = 1 if members > 1 else 0

    def swap(x, offset):
        return lax.ppermute(x, "ctx", [(j, j ^ offset) for j in range(n_ctx)])

    far = sorted((offset for offset in range(groups) if offset.bit_count() > 1), key=lambda offset: -offset.bit_count())
    near = [offset for offset in range(groups) if offset.bit_count() == 1]
    route = [(0, 0)] + [(offset, offset) for offset in far] + list(zip(near, reversed(near)))
    early, late = [*range(1 + len(far))], [*range(1 + len(far), groups)]

    def send(x, place):
        offset = [route[place][odd_one(j // members, j % members)] for j in range(n_ctx)]
        return lax.ppermute(x, "ctx", [(j, j ^ (offset[j] * members + cross)) for j in range(n_ctx)])

    kv_pack = (2 * per_group * rows + ID_ROWS, 2 * head_dim)
    q_pack = (per_group * rows, 2 * head_dim)

    def in_hbm(x):
        return pltpu.with_memory_space_constraint(x, pltpu.HBM)

    def pack(name, places, shape, turns, with_ids, sources):
        return pl.pallas_call(
            functools.partial(pack_kernel, [route[place] for place in places], members, turns, with_ids),
            out_shape=[pltpu.VMEM(shape, bf16)] * len(places),
            in_specs=[hbm] * (2 + len(sources)),
            out_specs=[vmem] * len(places),
            scratch_shapes=[
                pltpu.VMEM((len(sources), len(places), rows, per_group * head_dim), bf16),
                pltpu.SemaphoreType.DMA((len(sources), len(places))),
                pltpu.SMEM(block_order.shape, jnp.int32),
                pltpu.VMEM(clip_ids.shape, jnp.int32),
                pltpu.SemaphoreType.DMA((2,)),
            ],
            compiler_params=pltpu.CompilerParams(vmem_limit_bytes=16 * MIB),
            name=name,
        )(*map(in_hbm, (block_order, clip_ids) + sources))

    key_sources = (keys, tangent_keys, values, tangent_values)
    far_kv = pack("pack_far", early[1:], kv_pack, (True, False), True, key_sources)
    near_kv = pack("pack_near", [0, *late], kv_pack, (True, False), True, key_sources)
    kv = [near_kv[0], *far_kv, *near_kv[1:]]
    q = list(pack("pack_queries", range(groups), q_pack, (True,), False, (tangent_queries, queries)))

    weight, cot, staged = pl.pallas_call(
        stage_kernel,
        out_shape=[pltpu.VMEM(out_weight.shape, bf16), pltpu.VMEM(cotangent.shape, bf16), pltpu.VMEM((8, 128), jnp.float32)],
        in_specs=[hbm, hbm, vmem],
        out_specs=[vmem] * 3,
        scratch_shapes=[pltpu.SemaphoreType.DMA((2,))],
        compiler_params=pltpu.CompilerParams(vmem_limit_bytes=16 * MIB),
        name="stage",
    )(in_hbm(out_weight), in_hbm(cotangent), q[0])

    def exchange(sent):
        return [sent[0]] + [send(sent[place], place) for place in range(1, groups)]

    kv = exchange(kv)
    q = exchange(q)

    def merge(name, packs, after):
        places = len(packs)
        return pl.pallas_call(
            merge_kernel,
            out_shape=[
                jax.ShapeDtypeStruct((places * 2 * per_group * rows + places // 2 * rows, 2 * head_dim), bf16),
                jax.ShapeDtypeStruct((places * rows, 2 * head_dim), bf16),
            ],
            in_specs=[vmem] * (places + 1),
            out_specs=[vmem] * 2,
            compiler_params=pltpu.CompilerParams(vmem_limit_bytes=16 * MIB),
            name=name,
        )(*packs, after)

    merged_first, features_first = merge("merge_first", kv[: groups // 2], q[0])
    merged_last, features_last = merge("merge_last", kv[groups // 2 :], staged)
    others = [swap(merged, s) for s in range(1, members) for merged in (merged_first, merged_last)]
    arrived = pl.pallas_call(
        arrived_kernel,
        out_shape=jax.ShapeDtypeStruct((8, 128), jnp.float32),
        in_specs=[vmem] * len(early),
        out_specs=vmem,
        compiler_params=pltpu.CompilerParams(vmem_limit_bytes=16 * MIB),
        cost_estimate=pl.CostEstimate(flops=10**11, bytes_accessed=MIB, transcendentals=0),
        name="arrived",
    )(*(q[place] for place in early))

    def attend(name, places, *after):
        return pl.pallas_call(
            functools.partial(attend_kernel, groups, members, places, head_dim ** (-0.5)),
            out_shape=[jax.ShapeDtypeStruct((rows, per_group * head_dim), bf16)] * len(places),
            in_specs=[vmem] * (groups + 2 * members + len(places) + len(after)),
            out_specs=[vmem] * len(places),
            compiler_params=pltpu.CompilerParams(vmem_limit_bytes=24 * MIB),
            name=name,
        )(*kv, features_first, features_last, *others, *(q[place] for place in places), *after)

    done = dict(zip(early, attend("attend_early", early, arrived)))
    for place in early[1:]:
        done[place] = send(done[place], place)
    done.update(zip(late, attend("attend_late", late)))
    for place in late:
        done[place] = send(done[place], place)
    arrivals = [*early, *late]
    begun = None
    for place in arrivals[:-1]:
        begun = pl.pallas_call(
            functools.partial(part_kernel, members, route[place], 512),
            out_shape=jax.ShapeDtypeStruct((rows, width), jnp.float32),
            in_specs=[vmem] * (2 + (begun is not None)),
            out_specs=vmem,
            compiler_params=pltpu.CompilerParams(vmem_limit_bytes=16 * MIB),
            name=f"part{place}",
        )(done[place], weight, *([] if begun is None else [begun]))
    projected, grad = pl.pallas_call(
        functools.partial(project_kernel, members, route[arrivals[-1]], 512),
        out_shape=[jax.ShapeDtypeStruct((rows, width), jnp.float32), jax.ShapeDtypeStruct((1, width), jnp.float32)],
        in_specs=[vmem] * 4,
        out_specs=[vmem] * 2,
        compiler_params=pltpu.CompilerParams(vmem_limit_bytes=16 * MIB),
        name="project",
    )(done[arrivals[-1]], weight, begun, cot)
    branch = pl.pallas_call(
        branch_kernel,
        out_shape=jax.ShapeDtypeStruct((1, rows, width), bf16),
        in_specs=[vmem] * 2,
        out_specs=vmem,
        compiler_params=pltpu.CompilerParams(vmem_limit_bytes=16 * MIB),
        name="branch",
    )(projected, layer_scale[None, :])
    summed = exchange_sum(grad, [(s, 0) for s in reversed(range(1, members))])
    summed = exchange_sum(summed, [(offset + cross, 0) for offset in reversed(range(members, n_ctx, members))])
    factor = 1.0 / math.sqrt(n_ctx * n_dp * rows)
    offsets = [1 << k for k in range(n_dp.bit_length() - 1)]
    for offset in offsets:
        summed = exchange_sum(summed, [(cross, offset)], factor if offset == offsets[-1] else 1.0)
    return branch, summed[0]


def solution(mesh):
    tokens = P("dp", "ctx", None)
    in_specs = (tokens,) * 6 + (P("dp", "ctx"), P(), P(), P(), tokens)
    return jax.shard_map(local, mesh=mesh, in_specs=in_specs, out_specs=(tokens, P()), check_vma=False)
```
